256 devices in a mesh: orb: 64 (over y, z_lo, x), fft: 4 (over z_hi, core).
Axes of the slice: x: 4, y: 4, z: 8 (z_hi: 2, z_lo: 4; z = z_hi * 4 + z_lo), core: 2. Of those that a mesh axis runs over, the one named last changes fastest.
Arguments:
- orbitals: float32 [64, 96, 9216], P('orb', 'fft'), may hold values from -6 to 6
- sphere_depth: int32 [49, 96], replicated, may hold values from -1 to 23, as said below
Outputs:
- exchange_potential: float32 [64, 96, 9216], P('orb', 'fft')
The draws below stay inside these ranges and needn't reach their ends.
Inputs may be any that keep to these rules, and one draw needn't show every extreme that they name: sphere_depth[kx, p] belongs to the column of kx and the signed frequency of position p (p, or p - 96 from 48 on); each column keeps |kz| up to its own depth, never beyond the sphere kx^2 + ky^2 + kz^2 <= 23^2; the kept region is symmetric under ky -> -ky and kz -> -kz; column (0, 0) keeps |kz| up to 23; every column with kx > 23 or signed |ky| > 23 is -1.
All inputs are finite; a program needn't handle non-finite values.
Results may differ from the reference program's by a relative error of at most 0.0003.
Values sent between devices are 32-bit elements; how exact they have to be, the bound alone decides.
A program may use at most 64 MiB of HBM per device.

```python
import jax
import jax.numpy as jnp

NG = 96
CROP = 23
ORB_DEV = 1
STEPS = 2
BLOCKS = 64
NORB = 64


def draw_orbitals(key, part):
    key = jax.random.fold_in(key, 11)
    return jnp.clip(jax.random.normal(key, (NORB, NG, NG * NG), jnp.float32), -5.0, 5.0)


def draw_sphere_depth(key, part):
    key = jax.random.fold_in(key, 23)
    half_count = NG // 2 + 1
    kx_range = jnp.arange(half_count, dtype=jnp.int32)[:, None, None]
    ky_index = jnp.arange(NG, dtype=jnp.int32)
    ky_signed = jnp.where(2 * ky_index >= NG, ky_index - NG, ky_index)
    ky_range = ky_signed[None, :, None]
    kz_range = jnp.arange(half_count, dtype=jnp.int32)[None, None, :]
    inside = kx_range * kx_range + ky_range * ky_range + kz_range * kz_range <= CROP * CROP
    base_depth = jnp.sum(inside.astype(jnp.int32), axis=2) - 1
    cut_table = jax.random.randint(key, (half_count, half_count), 0, 4)
    cut_full = cut_table[:, jnp.abs(ky_signed)]
    centre = (kx_range[:, :, 0] == 0) & (ky_signed[None, :] == 0)
    cut_full = jnp.where(centre, 0, cut_full)
    depth = jnp.where(base_depth >= 0, jnp.maximum(base_depth - cut_full, -1), -1)
    return depth.astype(jnp.int32)


def setup_inputs(seed: int = 0) -> dict:
    keys = jax.random.split(jax.random.key(seed), 3)
    orbitals = draw_orbitals(jax.random.fold_in(keys[2], 71), 0)
    sphere_depth = draw_sphere_depth(jax.random.fold_in(keys[2], 71), 0)
    return {"orbitals": orbitals, "sphere_depth": sphere_depth}


def signed_range(length):
    index_row = jnp.arange(length, dtype=jnp.int32)
    return jnp.where(2 * index_row >= length, index_row - length, index_row)


def coulomb_kernel(sphere_depth):
    kz_range = signed_range(NG)[:, None, None]
    ky_range = signed_range(NG)[None, :, None]
    kx_range = jnp.arange(NG // 2 + 1, dtype=jnp.int32)[None, None, :]
    depth_table = jnp.transpose(sphere_depth)[None, :, :]
    square = kx_range * kx_range + ky_range * ky_range + kz_range * kz_range
    inside = (jnp.abs(kz_range) <= depth_table) & (square > 0)
    scale = 0.1 * NG ** 1.5
    return jnp.where(inside, scale / jnp.maximum(square.astype(jnp.float32), 1.0), 0.0).astype(jnp.float32)


def potential(density, kernel):
    grid_cells = density.reshape(density.shape[0], NG, NG, NG)
    spectrum = jnp.fft.rfftn(grid_cells, axes=(1, 2, 3))
    field = jnp.fft.irfftn(spectrum * kernel, s=(NG, NG, NG), axes=(1, 2, 3))
    return field.reshape(density.shape).astype(jnp.float32)


def reference(orbitals, sphere_depth):
    kernel = coulomb_kernel(sphere_depth)
    blocks = orbitals.reshape(BLOCKS, ORB_DEV, NG, NG * NG)
    result = jnp.zeros(blocks.shape, jnp.float32)
    for cycle_step in range(STEPS):
        partner = jnp.roll(blocks, cycle_step, axis=0)
        returned = jnp.zeros(blocks.shape, jnp.float32)
        for left_index in range(ORB_DEV):
            for right_index in range(ORB_DEV):
                pair_field = potential(blocks[:, left_index] * partner[:, right_index], kernel)
                result = result.at[:, left_index].add(partner[:, right_index] * pair_field)
                if cycle_step > 0:
                    returned = returned.at[:, right_index].add(blocks[:, left_index] * pair_field)
        if cycle_step > 0:
            result = result + jnp.roll(returned, -cycle_step, axis=0)
    return result.reshape(NORB, NG, NG * NG)
```

```python
import functools
import math

import jax
import jax.numpy as jnp
import ml_dtypes
import numpy as np
from jax import lax
from jax.experimental import pallas as pl
from jax.experimental.pallas import tpu as pltpu
from jax.sharding import PartitionSpec as P

NG = 96
PLANES = 24
HALF = 24
ROWS = 48
SPEC = HALF // 2 * ROWS
COULOMB = 0.1
BF = jnp.bfloat16
F32 = jnp.float32
MESH = pl.DeviceIdType.MESH


def signed_order(count):
    place = np.arange(count)
    size = (place + 1) // 2
    return np.where(place % 2 == 1, size, -size)


def angle(a, b):
    return 2.0 * math.pi / NG * (np.outer(a, b) % NG)


def split_table(table):
    high = table.astype(ml_dtypes.bfloat16)
    low = (table - high.astype(np.float64)).astype(ml_dtypes.bfloat16)
    return high, low


def make_tables():
    grid = np.arange(NG)
    ky = np.arange(HALF)
    a = angle(ky, grid)
    hi, lo = split_table(np.concatenate([np.cos(a), -np.sin(a)], 0))
    t1 = np.block([[hi, hi], [lo, lo]])

    kx = signed_order(47)
    a = np.zeros((128, 64))
    c, s = np.zeros((128, 64)), np.zeros((128, 64))
    c[:NG, :47] = np.cos(angle(grid, kx))
    s[:NG, :47] = np.sin(angle(grid, kx))
    hi, lo = split_table(np.block([[c, -s], [s, c]]))
    t2 = np.concatenate([hi, lo], 1)
    hi, lo = split_table(np.block([[c.T, s.T], [-s.T, c.T]]))
    t2b = np.concatenate([hi, hi, lo], 0)

    weight = np.where(ky == 0, 1.0, 2.0) / float(NG**3)
    a = angle(grid, ky)
    hi, lo = split_table(np.concatenate([np.cos(a) * weight, -np.sin(a) * weight], 1))
    t1b = np.concatenate([hi, hi, lo], 1)

    kz = signed_order(ROWS)
    t3, t3b = [], []
    for slab in range(NG // PLANES):
        z = slab * PLANES + np.arange(PLANES)
        a = angle(kz, z)
        hi, lo = split_table(np.concatenate([np.cos(a), np.sin(a)], 0))
        t3.append(np.concatenate([hi, hi, lo, lo], 1))
        a = angle(z, kz)
        hi, lo = split_table(np.concatenate([np.cos(a), np.sin(a)], 0))
        t3b.append(np.concatenate([hi, hi, lo], 1))
    pick = np.zeros((HALF, 128), np.float32)
    for lane in range(128):
        if lane % 64 < 47:
            pick[abs(kx[lane % 64]), lane] = 1.0
    return t1, t2, np.stack(t3), np.stack(t3b), t2b, t1b, pick


def lanes(rows):
    return lax.broadcasted_iota(jnp.int32, (rows, 128), 1)


def split(value):
    high = value.astype(BF)
    return high, (value - high.astype(F32)).astype(BF)


def dot(a, b):
    return jnp.dot(a, b, preferred_element_type=F32)


def spread(raw, grid, tile):
    row = tile * 8
    lane = lanes(8)

    @pl.loop(0, NG // 4)
    def _(group):
        block = raw[pl.ds(row, 8), pl.ds(pl.multiple_of(group * 384, 128), 384)]
        t0, t1, t2 = block[:, :128], block[:, 128:256], block[:, 256:]
        pieces = (
            t0,
            pltpu.roll(jnp.where(lane >= 96, t0, t1), 32, 1),
            pltpu.roll(jnp.where(lane >= 64, t1, t2), 64, 1),
            pltpu.roll(t2, 96, 1),
        )
        for j, piece in enumerate(pieces):
            grid[pl.ds(row * NG + group * 4 + j, 8, stride=NG), :] = piece


def gather(grid, out):
    lane = lanes(PLANES)

    @pl.loop(0, NG // 4)
    def _(group):
        a = [grid[pl.ds(group * 4 + j, PLANES, stride=NG), :] for j in range(4)]
        r1, r2, r3 = pltpu.roll(a[1], 96, 1), pltpu.roll(a[2], 64, 1), pltpu.roll(a[3], 32, 1)
        start = pl.multiple_of(group * 384, 128)
        out[:, pl.ds(start, 128)] = jnp.where(lane < 96, a[0], r1)
        out[:, pl.ds(start + 128, 128)] = jnp.where(lane < 64, r1, r2)
        out[:, pl.ds(start + 256, 128)] = jnp.where(lane < 32, r2, r3)


def forward_y(left, right, t1, u, first, count):
    @pl.loop(first, first + count)
    def _(pair):
        rows = pl.ds(pl.multiple_of(pair * 2 * NG, 2 * NG), 2 * NG)
        hi, lo = split(left[rows, :] * right[rows, :])
        stacked = jnp.concatenate(
            [
                jnp.concatenate([hi[:NG], hi[NG:]], 1),
                jnp.concatenate([lo[:NG], lo[NG:]], 1),
            ],
            0,
        )
        o = dot(t1[...], stacked)
        o = o[:48] + o[48:]
        for t in range(2):
            where = pl.ds(pair * 2 + t, HALF, stride=PLANES)
            u.at[0][where, :] = o[:24, 128 * t : 128 * t + 128]
            u.at[1][where, :] = o[24:, 128 * t : 128 * t + 128]


def forward_x(u, t2, f):
    @pl.loop(0, 4)
    def _(block):
        rows = pl.ds(pl.multiple_of(block * 144, 144), 144)
        hi, lo = split(jnp.concatenate([u[0, rows, :], u[1, rows, :]], 1))
        o = dot(hi, t2[...])
        f[rows, :] = o[:, :128] + o[:, 128:] + dot(lo, t2[:, :128])


def forward_z(f, t3, coulomb, spectrum):
    sign = jnp.where(lanes(ROWS) < 64, 1.0, -1.0)

    @pl.loop(0, HALF // 2)
    def _(pair):
        v = f[pl.ds(pl.multiple_of(pair * 48, 48), 48), :]
        v = jnp.concatenate([v[:24], v[24:]], 1)
        hi = v.astype(BF).astype(F32)
        lo = v - hi
        o = dot(t3[...], jnp.concatenate([hi, lo, hi, lo], 0).astype(BF))
        rows = pl.ds(pl.multiple_of(pair * ROWS, ROWS), ROWS)
        for t in range(2):
            part = o[:, 128 * t : 128 * t + 128]
            part = part[:48] + sign * pltpu.roll(part[48:], 64, 1)
            spectrum[t, rows, :] = part * coulomb[t, rows, :]


def backward_z(spectrum, t3b, f):
    sign = jnp.where(lanes(PLANES) < 64, -1.0, 1.0)

    @pl.loop(0, HALF // 2)
    def _(pair):
        rows = pl.ds(pl.multiple_of(pair * ROWS, ROWS), ROWS)
        hi, lo = split(jnp.concatenate([spectrum[0, rows, :], spectrum[1, rows, :]], 1))
        o = dot(t3b[...], jnp.concatenate([hi, lo, hi], 0))
        for t in range(2):
            part = o[:, 128 * t : 128 * t + 128]
            f[pl.ds(pl.multiple_of(pair * 48 + 24 * t, 24), 24), :] = part[:24] + sign * pltpu.roll(
                part[24:], 64, 1
            )


def backward_x(f, t2b, u):
    @pl.loop(0, 4)
    def _(block):
        rows = pl.ds(pl.multiple_of(block * 144, 144), 144)
        hi, lo = split(f[rows, :])
        o = dot(jnp.concatenate([hi, lo], 1), t2b[:256, :]) + dot(hi, t2b[256:, :])
        u[0, rows, :] = o[:, :128]
        u[1, rows, :] = o[:, 128:]


def backward_y(u, t1b, orbital, total, fresh):
    @pl.loop(0, PLANES // 2)
    def _(pair):
        parts = []
        for t in range(2):
            where = pl.ds(pair * 2 + t, HALF, stride=PLANES)
            parts.append(jnp.concatenate([u.at[0][where, :], u.at[1][where, :]], 0))
        hi, lo = split(jnp.concatenate(parts, 1))
        v = dot(t1b[...], jnp.concatenate([hi, lo, hi], 0))
        for t in range(2):
            rows = pl.ds(pl.multiple_of((pair * 2 + t) * NG, NG), NG)
            term = orbital[rows, :] * v[:, 128 * t : 128 * t + 128]
            total[rows, :] = term if fresh else total[rows, :] + term


def fill_coulomb(depth, pick, coulomb, limits):
    kept = depth[...].astype(F32)[:HALF] + 1.0
    limits[...] = lax.dot_general(
        kept, pick[...], (((0,), (0,)), ((), ())), preferred_element_type=F32
    ) - 1.0
    lane = lax.broadcasted_iota(jnp.int32, (ROWS, 128), 1) % 64
    row = lax.broadcasted_iota(jnp.int32, (ROWS, 128), 0)
    kx, kz = (lane + 1) // 2, (row + 1) // 2
    square = (kx * kx + kz * kz).astype(F32)
    size = kz.astype(F32)

    @pl.loop(0, HALF // 2)
    def _(pair):
        for t in range(2):
            ky = pair * 2 + t
            whole = square + (ky * ky).astype(F32)
            inside = (size <= limits[pl.ds(ky, 1), :]) & (whole > 0.5)
            coulomb[t, pl.ds(pl.multiple_of(pair * ROWS, ROWS), ROWS), :] = jnp.where(
                inside, COULOMB * NG**1.5 / jnp.maximum(whole, 1.0), 0.0
            )


def kernel(
    own, depth, t1, t2, t3, t3b, t2b, t1b, pick, out,
    raw, grids, total, u, f, coulomb, limits,
    spectra, arrived, summed, crossed, fields,
    phi_send, phi_recv, half_send, half_recv, far_send, far_recv, give_send, give_recv,
):
    orb, fft = lax.axis_index("orb"), lax.axis_index("fft")
    blocks = lax.axis_size("orb")
    core = fft % 2
    other = fft + 1 - 2 * core
    far = (fft + 2) % 4
    near = (orb + blocks - 1 + 2 * core) % blocks
    back = (orb + 1 - 2 * core) % blocks

    barrier = pltpu.get_barrier_semaphore()
    for peer in ((near, fft), (back, fft), (orb, other), (near, other), (orb, far)):
        pl.semaphore_signal(barrier, inc=1, device_id=peer, device_id_type=MESH)
    pl.semaphore_wait(barrier, 5)

    def send(src, dst, send_sem, recv_sem, peer):
        return pltpu.make_async_remote_copy(
            src_ref=src, dst_ref=dst, send_sem=send_sem, recv_sem=recv_sem,
            device_id=peer, device_id_type=MESH,
        )

    def orbital_copy(phase, tile, peer):
        rows = pl.ds(tile * 8, 8)
        return send(own.at[rows], raw.at[phase, rows], phi_send.at[phase, tile],
                    phi_recv.at[phase, tile], peer)

    first = [orbital_copy(0, tile, (back, fft)) for tile in range(3)]
    second = [orbital_copy(1, tile, (near, fft)) for tile in range(3)]
    for copy in first:
        copy.start()

    mine, mate, after = grids.at[0], grids.at[1], grids.at[2]
    fill_coulomb(depth, pick, coulomb, limits)
    for tile in range(3):
        spread(own, mine, tile)

    halves = [
        send(spectra.at[pair, 1 - core], arrived.at[pair], half_send.at[pair], half_recv.at[pair], peer)
        for pair, peer in enumerate(((orb, other), (near, other)))
    ]
    fars = [
        send(summed.at[pair], crossed.at[pair], far_send.at[pair], far_recv.at[pair], (orb, far))
        for pair in range(2)
    ]

    def give(slot, field, peer):
        return send(fields.at[0 if slot == 0 else 1, core], fields.at[field, core],
                    give_send.at[slot], give_recv.at[slot], peer)

    gives = [give(0, 0, (orb, other)), give(1, 1, (near, other)), give(2, 2, (orb, other)),
             give(3, 2, (near, fft))]

    forward_y(mine, mine, t1, u, 0, 12)
    forward_x(u, t2, f)
    forward_z(f, t3, coulomb, spectra.at[0])
    halves[0].start()
    halves[0].wait_recv()
    summed[0] = spectra[0, core] + arrived[0]
    fars[0].start()

    for tile in range(3):
        first[tile].wait_recv()
        spread(raw.at[0], mate, tile)
        forward_y(mine, mate, t1, u, tile * 4, 4)
    for copy in first:
        copy.wait_send()
    forward_x(u, t2, f)
    forward_z(f, t3, coulomb, spectra.at[1])
    halves[1].start()
    for copy in second:
        copy.start()

    fars[0].wait_recv()
    fields[0, core] = summed[0] + crossed[0]
    gives[0].start()

    halves[1].wait_recv()
    summed[1] = spectra[1, core] + arrived[1]
    fars[1].start()

    gives[0].wait_recv()
    backward_z(fields.at[0], t3b, f)
    backward_x(f, t2b, u)
    backward_y(u, t1b, mine, total, True)

    for tile in range(3):
        second[tile].wait_recv()
        spread(raw.at[1], after, tile)

    fars[1].wait_recv()
    fields[1, core] = summed[1] + crossed[1]
    for copy in gives[1:]:
        copy.start()
    gives[1].wait_recv()
    backward_z(fields.at[1], t3b, f)
    backward_x(f, t2b, u)
    backward_y(u, t1b, mate, total, False)
    gives[2].wait_recv()
    gives[3].wait_recv()
    backward_z(fields.at[2], t3b, f)
    backward_x(f, t2b, u)
    backward_y(u, t1b, after, total, False)
    gather(total, out)
    for copy in halves + fars + gives + second:
        copy.wait_send()


def shards(orbitals, sphere_depth):
    t1, t2, t3, t3b, t2b, t1b, pick = make_tables()
    slab = lax.axis_index("fft")
    t3 = lax.dynamic_index_in_dim(jnp.asarray(t3), slab, 0, keepdims=False)
    t3b = lax.dynamic_index_in_dim(jnp.asarray(t3b), slab, 0, keepdims=False)
    vmem = pl.BlockSpec(memory_space=pltpu.VMEM)
    cells = NG * NG
    dma = pltpu.SemaphoreType.DMA
    result = pl.pallas_call(
        kernel,
        out_shape=jax.ShapeDtypeStruct((PLANES, cells), F32),
        in_specs=[vmem] * 9,
        out_specs=vmem,
        scratch_shapes=[
            pltpu.VMEM((2, PLANES, cells), F32),
            pltpu.VMEM((3, PLANES * NG, 128), F32),
            pltpu.VMEM((PLANES * NG, 128), F32),
            pltpu.VMEM((2, HALF * PLANES, 128), F32),
            pltpu.VMEM((HALF * PLANES, 128), F32),
            pltpu.VMEM((2, SPEC, 128), F32),
            pltpu.VMEM((NG, 128), F32),
            pltpu.VMEM((2, 2, SPEC, 128), F32),
            pltpu.VMEM((2, SPEC, 128), F32),
            pltpu.VMEM((2, SPEC, 128), F32),
            pltpu.VMEM((2, SPEC, 128), F32),
            pltpu.VMEM((3, 2, SPEC, 128), F32),
            dma((2, 3)), dma((2, 3)), dma((2,)), dma((2,)), dma((2,)), dma((2,)), dma((4,)), dma((4,)),
        ],
        compiler_params=pltpu.CompilerParams(
            collective_id=0, has_side_effects=True, vmem_limit_bytes=40 << 20
        ),
        cost_estimate=pl.CostEstimate(flops=10**9, bytes_accessed=4 * 10**6, transcendentals=0),
    )(
        orbitals.reshape(PLANES, cells), sphere_depth,
        jnp.asarray(t1), jnp.asarray(t2), t3, t3b,
        jnp.asarray(t2b), jnp.asarray(t1b), jnp.asarray(pick),
    )
    return result.reshape(orbitals.shape)


def solution(mesh):
    placed = (P("orb", "fft", None), P())
    return jax.shard_map(
        shards, mesh=mesh, in_specs=placed, out_specs=P("orb", "fft", None), check_vma=False
    )
```

```python
import functools
import math

import jax
import jax.numpy as jnp
import ml_dtypes
import numpy as np
from jax import lax
from jax.experimental import pallas as pl
from jax.experimental.pallas import tpu as pltpu
from jax.sharding import PartitionSpec as P

NG = 96
PLANES = 24
HALF = 24
ROWS = 48
CROP = 23
UNROLL = dict(spread=4, gather=4, forward_y=4, forward_x=2, backward_x=2, backward_y=4)
COULOMB = 0.1
BF = jnp.bfloat16
F32 = jnp.float32
MESH = pl.DeviceIdType.MESH


def signed_order(count):
    place = np.arange(count)
    size = (place + 1) // 2
    return np.where(place % 2 == 1, size, -size)


def angle(a, b):
    return 2.0 * math.pi / NG * (np.outer(a, b) % NG)


def half_of(ky):
    return int(ky % 4 in (1, 2))


def pack_blocks():
    place, most = {}, 0
    for half in range(2):
        blocks = []
        for ky in range(HALF):
            for m in range(ROWS // 8):
                left = CROP**2 - ky**2 - (4 * m) ** 2
                if half_of(ky) == half and left >= 0:
                    blocks.append((2 * math.isqrt(left) + 1, ky, m))
        used = []
        for width, ky, m in sorted(blocks, key=lambda b: -b[0]):
            for tile, filled in enumerate(used):
                if filled + width <= 64:
                    break
            else:
                tile = len(used)
                used.append(0)
            place[ky, m] = (half, tile, used[tile], width)
            used[tile] += width
        most = max(most, len(used))
    return place, most


PLACE, TILES = pack_blocks()
PACKED = TILES * 8


def split_table(table):
    high = table.astype(ml_dtypes.bfloat16)
    low = (table - high.astype(np.float64)).astype(ml_dtypes.bfloat16)
    return high, low


def make_tables():
    grid = np.arange(NG)
    ky = np.arange(HALF)
    a = angle(ky, grid)
    hi, lo = split_table(np.concatenate([np.cos(a), -np.sin(a)], 0))
    t1 = np.block([[hi, hi], [lo, lo]])

    kx = signed_order(47)
    a = np.zeros((128, 64))
    c, s = np.zeros((128, 64)), np.zeros((128, 64))
    c[:NG, :47] = np.cos(angle(grid, kx))
    s[:NG, :47] = np.sin(angle(grid, kx))
    hi, lo = split_table(np.block([[c, -s], [s, c]]))
    t2 = np.concatenate([hi, lo], 1)
    hi, lo = split_table(np.block([[c.T, s.T], [-s.T, c.T]]))
    t2b = np.concatenate([hi, hi, lo], 0)

    weight = np.where(ky == 0, 1.0, 2.0) / float(NG**3)
    a = angle(grid, ky)
    hi, lo = split_table(np.concatenate([np.cos(a) * weight, -np.sin(a) * weight], 1))
    t1b = np.concatenate([hi, hi, lo], 1)

    kz = signed_order(ROWS)
    t3, t3b = [], []
    for slab in range(NG // PLANES):
        z = slab * PLANES + np.arange(PLANES)
        a = angle(kz, z)
        hi, lo = split_table(np.concatenate([np.cos(a), np.sin(a)], 0))
        t3.append(np.concatenate([hi, hi, lo, lo], 1))
        a = angle(z, kz)
        hi, lo = split_table(np.concatenate([np.cos(a), np.sin(a)], 0))
        t3b.append(np.concatenate([hi, hi, lo], 1))
    pick = np.zeros((HALF, 128), np.float32)
    for lane in range(128):
        if lane % 64 < 47:
            pick[abs(kx[lane % 64]), lane] = 1.0
    return t1, t2, np.stack(t3), np.stack(t3b), t2b, t1b, pick


def lanes(rows):
    return lax.broadcasted_iota(jnp.int32, (rows, 128), 1)


def split(value):
    high = value.astype(BF)
    return high, (value - high.astype(F32)).astype(BF)


def dot(a, b):
    return jnp.dot(a, b, preferred_element_type=F32)


def spread(raw, grid, tile):
    row = tile * 8
    lane = lanes(8)

    @pl.loop(0, NG // 4, unroll=UNROLL["spread"])
    def _(group):
        block = raw[pl.ds(row, 8), pl.ds(pl.multiple_of(group * 384, 128), 384)]
        t0, t1, t2 = block[:, :128], block[:, 128:256], block[:, 256:]
        pieces = (
            t0,
            pltpu.roll(jnp.where(lane >= 96, t0, t1), 32, 1),
            pltpu.roll(jnp.where(lane >= 64, t1, t2), 64, 1),
            pltpu.roll(t2, 96, 1),
        )
        for j, piece in enumerate(pieces):
            grid[pl.ds(row * NG + group * 4 + j, 8, stride=NG), :] = piece


def gather(grid, out):
    lane = lanes(PLANES)

    @pl.loop(0, NG // 4, unroll=UNROLL["gather"])
    def _(group):
        a = [grid[pl.ds(group * 4 + j, PLANES, stride=NG), :] for j in range(4)]
        r1, r2, r3 = pltpu.roll(a[1], 96, 1), pltpu.roll(a[2], 64, 1), pltpu.roll(a[3], 32, 1)
        start = pl.multiple_of(group * 384, 128)
        out[:, pl.ds(start, 128)] = jnp.where(lane < 96, a[0], r1)
        out[:, pl.ds(start + 128, 128)] = jnp.where(lane < 64, r1, r2)
        out[:, pl.ds(start + 256, 128)] = jnp.where(lane < 32, r2, r3)


def forward_y(left, right, t1, u, first, count):
    @pl.loop(first, first + count, unroll=UNROLL["forward_y"])
    def _(pair):
        rows = pl.ds(pl.multiple_of(pair * 2 * NG, 2 * NG), 2 * NG)
        hi, lo = split(left[rows, :] * right[rows, :])
        stacked = jnp.concatenate(
            [
                jnp.concatenate([hi[:NG], hi[NG:]], 1),
                jnp.concatenate([lo[:NG], lo[NG:]], 1),
            ],
            0,
        )
        o = dot(t1[...], stacked)
        o = o[:48] + o[48:]
        for t in range(2):
            where = pl.ds(pair * 2 + t, HALF, stride=PLANES)
            u.at[0][where, :] = o[:24, 128 * t : 128 * t + 128]
            u.at[1][where, :] = o[24:, 128 * t : 128 * t + 128]


def forward_x(u, t2, f):
    @pl.loop(0, 4, unroll=UNROLL["forward_x"])
    def _(block):
        rows = pl.ds(pl.multiple_of(block * 144, 144), 144)
        hi, lo = split(jnp.concatenate([u[0, rows, :], u[1, rows, :]], 1))
        o = dot(hi, t2[...])
        f[rows, :] = o[:, :128] + o[:, 128:] + dot(lo, t2[:, :128])


def forward_z(f, t3, coulomb, spectrum):
    sign = jnp.where(lanes(ROWS) < 64, 1.0, -1.0)
    written = set()
    for pair in range(HALF // 2):
        v = f[pl.ds(pair * 48, 48), :]
        v = jnp.concatenate([v[:24], v[24:]], 1)
        hi = v.astype(BF).astype(F32)
        lo = v - hi
        o = dot(t3[...], jnp.concatenate([hi, lo, hi, lo], 0).astype(BF))
        for t in range(2):
            ky = pair * 2 + t
            part = o[:, 128 * t : 128 * t + 128]
            part = part[:48] + sign * pltpu.roll(part[48:], 64, 1)
            part = part * coulomb[pl.ds(ky * ROWS, ROWS), :]
            for m in range(ROWS // 8):
                if (ky, m) not in PLACE:
                    continue
                half, tile, shift, _ = PLACE[ky, m]
                block = part[8 * m : 8 * m + 8]
                if shift:
                    block = pltpu.roll(block, shift, 1)
                rows = pl.ds(tile * 8, 8)
                if (half, tile) in written:
                    block = block + spectrum[half, rows, :]
                spectrum[half, rows, :] = block
                written.add((half, tile))
    for half in range(2):
        for tile in range(TILES):
            if (half, tile) not in written:
                spectrum[half, pl.ds(tile * 8, 8), :] = jnp.zeros((8, 128), F32)


def backward_z(spectrum, t3b, f):
    sign = jnp.where(lanes(PLANES) < 64, -1.0, 1.0)
    lane = lanes(8) % 64
    none = jnp.zeros((8, 128), F32)

    def unpacked(ky):
        blocks = []
        for m in range(ROWS // 8):
            if (ky, m) not in PLACE:
                blocks.append(none)
                continue
            half, tile, shift, width = PLACE[ky, m]
            block = spectrum[half, pl.ds(tile * 8, 8), :]
            if shift:
                block = pltpu.roll(block, 128 - shift, 1)
            blocks.append(jnp.where(lane < width, block, 0.0))
        return jnp.concatenate(blocks, 0)

    for pair in range(HALF // 2):
        hi, lo = split(jnp.concatenate([unpacked(pair * 2), unpacked(pair * 2 + 1)], 1))
        o = dot(t3b[...], jnp.concatenate([hi, lo, hi], 0))
        for t in range(2):
            part = o[:, 128 * t : 128 * t + 128]
            f[pl.ds(pair * 48 + 24 * t, 24), :] = part[:24] + sign * pltpu.roll(part[24:], 64, 1)


def backward_x(f, t2b, u):
    @pl.loop(0, 4, unroll=UNROLL["backward_x"])
    def _(block):
        rows = pl.ds(pl.multiple_of(block * 144, 144), 144)
        hi, lo = split(f[rows, :])
        o = dot(jnp.concatenate([hi, lo], 1), t2b[:256, :]) + dot(hi, t2b[256:, :])
        u[0, rows, :] = o[:, :128]
        u[1, rows, :] = o[:, 128:]


def backward_y(u, t1b, orbital, total, fresh):
    @pl.loop(0, PLANES // 2, unroll=UNROLL["backward_y"])
    def _(pair):
        parts = []
        for t in range(2):
            where = pl.ds(pair * 2 + t, HALF, stride=PLANES)
            parts.append(jnp.concatenate([u.at[0][where, :], u.at[1][where, :]], 0))
        hi, lo = split(jnp.concatenate(parts, 1))
        v = dot(t1b[...], jnp.concatenate([hi, lo, hi], 0))
        for t in range(2):
            rows = pl.ds(pl.multiple_of((pair * 2 + t) * NG, NG), NG)
            term = orbital[rows, :] * v[:, 128 * t : 128 * t + 128]
            total[rows, :] = term if fresh else total[rows, :] + term


def fill_coulomb(depth, pick, coulomb, limits):
    kept = depth[...].astype(F32)[:HALF] + 1.0
    limits[...] = lax.dot_general(
        kept, pick[...], (((0,), (0,)), ((), ())), preferred_element_type=F32
    ) - 1.0
    lane = lax.broadcasted_iota(jnp.int32, (ROWS, 128), 1) % 64
    row = lax.broadcasted_iota(jnp.int32, (ROWS, 128), 0)
    kx, kz = (lane + 1) // 2, (row + 1) // 2
    square = (kx * kx + kz * kz).astype(F32)
    size = kz.astype(F32)

    @pl.loop(0, HALF, unroll=4)
    def _(ky):
        whole = square + (ky * ky).astype(F32)
        inside = (size <= limits[pl.ds(ky, 1), :]) & (whole > 0.5)
        coulomb[pl.ds(pl.multiple_of(ky * ROWS, ROWS), ROWS), :] = jnp.where(
            inside, COULOMB * NG**1.5 / jnp.maximum(whole, 1.0), 0.0
        )


def kernel(
    own_hbm, depth_hbm, t1_hbm, t2_hbm, t3_hbm, t3b_hbm, t2b_hbm, t1b_hbm, pick_hbm, out,
    own, depth, t1, t2, t3, t3b, t2b, t1b, pick, load_sem, raw, grids, total, u, f, coulomb, limits,
    spectra, arrived, summed, crossed, fields,
    phi_send, phi_recv, half_send, half_recv, far_send, far_recv, give_send, give_recv,
):
    orb, fft = lax.axis_index("orb"), lax.axis_index("fft")
    blocks = lax.axis_size("orb")
    core = fft % 2
    other = fft + 1 - 2 * core
    far = (fft + 2) % 4
    near = (orb + blocks - 1 + 2 * core) % blocks
    back = (orb + 1 - 2 * core) % blocks

    loads = [
        pltpu.make_async_copy(src, dst, load_sem.at[place])
        for place, (src, dst) in enumerate((
            (own_hbm, own), (depth_hbm, depth), (pick_hbm, pick), (t1_hbm, t1), (t2_hbm, t2),
            (t3_hbm.at[fft], t3), (t3b_hbm.at[fft], t3b), (t2b_hbm, t2b), (t1b_hbm, t1b),
        ))
    ]
    for load in loads:
        load.start()

    barrier = pltpu.get_barrier_semaphore()
    for peer in ((near, fft), (back, fft), (orb, other), (near, other), (orb, far)):
        pl.semaphore_signal(barrier, inc=1, device_id=peer, device_id_type=MESH)
    pl.semaphore_wait(barrier, 5)

    def send(src, dst, send_sem, recv_sem, peer):
        return pltpu.make_async_remote_copy(
            src_ref=src, dst_ref=dst, send_sem=send_sem, recv_sem=recv_sem,
            device_id=peer, device_id_type=MESH,
        )

    def orbital_copy(phase, tile, peer):
        rows = pl.ds(tile * 8, 8)
        return send(own_hbm.at[rows], raw.at[phase, rows], phi_send.at[phase, tile],
                    phi_recv.at[phase, tile], peer)

    first = [orbital_copy(0, tile, (back, fft)) for tile in range(3)]
    second = [orbital_copy(1, tile, (near, fft)) for tile in range(3)]
    for copy in first:
        copy.start()

    mine, mate, after = grids.at[0], grids.at[1], grids.at[2]
    for load in loads:
        load.wait()
    fill_coulomb(depth, pick, coulomb, limits)
    for tile in range(3):
        spread(own, mine, tile)

    halves = [
        send(spectra.at[pair, 1 - core], arrived.at[pair], half_send.at[pair], half_recv.at[pair], peer)
        for pair, peer in enumerate(((orb, other), (near, other)))
    ]
    fars = [
        send(summed.at[pair], crossed.at[pair], far_send.at[pair], far_recv.at[pair], (orb, far))
        for pair in range(2)
    ]

    def give(slot, field, peer):
        return send(fields.at[0 if slot == 0 else 1, core], fields.at[field, core],
                    give_send.at[slot], give_recv.at[slot], peer)

    gives = [give(0, 0, (orb, other)), give(1, 1, (near, other)), give(2, 2, (orb, other)),
             give(3, 2, (near, fft))]

    forward_y(mine, mine, t1, u, 0, 12)
    forward_x(u, t2, f)
    forward_z(f, t3, coulomb, spectra.at[0])
    halves[0].start()
    halves[0].wait_recv()
    summed[0] = spectra[0, core] + arrived[0]
    fars[0].start()

    for tile in range(3):
        first[tile].wait_recv()
        spread(raw.at[0], mate, tile)
        forward_y(mine, mate, t1, u, tile * 4, 4)
    for copy in first:
        copy.wait_send()
    forward_x(u, t2, f)
    forward_z(f, t3, coulomb, spectra.at[1])
    halves[1].start()
    for copy in second:
        copy.start()

    fars[0].wait_recv()
    fields[0, core] = summed[0] + crossed[0]
    gives[0].start()

    halves[1].wait_recv()
    summed[1] = spectra[1, core] + arrived[1]
    fars[1].start()

    gives[0].wait_recv()
    backward_z(fields.at[0], t3b, f)
    backward_x(f, t2b, u)
    backward_y(u, t1b, mine, total, True)

    for tile in range(3):
        second[tile].wait_recv()
        spread(raw.at[1], after, tile)

    fars[1].wait_recv()
    fields[1, core] = summed[1] + crossed[1]
    for copy in gives[1:]:
        copy.start()
    gives[1].wait_recv()
    backward_z(fields.at[1], t3b, f)
    backward_x(f, t2b, u)
    backward_y(u, t1b, mate, total, False)
    gives[2].wait_recv()
    gives[3].wait_recv()
    backward_z(fields.at[2], t3b, f)
    backward_x(f, t2b, u)
    backward_y(u, t1b, after, total, False)
    gather(total, out)
    for copy in halves + fars + gives + second:
        copy.wait_send()


def shards(orbitals, sphere_depth):
    t1, t2, t3, t3b, t2b, t1b, pick = make_tables()
    vmem = pl.BlockSpec(memory_space=pltpu.VMEM)
    cells = NG * NG
    dma = pltpu.SemaphoreType.DMA
    result = pl.pallas_call(
        kernel,
        out_shape=jax.ShapeDtypeStruct((PLANES, cells), F32),
        in_specs=[pl.BlockSpec(memory_space=pltpu.HBM)] * 9,
        out_specs=vmem,
        scratch_shapes=[
            pltpu.VMEM((PLANES, cells), F32),
            pltpu.VMEM(sphere_depth.shape, jnp.int32),
            pltpu.VMEM(t1.shape, BF),
            pltpu.VMEM(t2.shape, BF),
            pltpu.VMEM(t3.shape[1:], BF),
            pltpu.VMEM(t3b.shape[1:], BF),
            pltpu.VMEM(t2b.shape, BF),
            pltpu.VMEM(t1b.shape, BF),
            pltpu.VMEM(pick.shape, F32),
            dma((9,)),
            pltpu.VMEM((2, PLANES, cells), F32),
            pltpu.VMEM((3, PLANES * NG, 128), F32),
            pltpu.VMEM((PLANES * NG, 128), F32),
            pltpu.VMEM((2, HALF * PLANES, 128), F32),
            pltpu.VMEM((HALF * PLANES, 128), F32),
            pltpu.VMEM((HALF * ROWS, 128), F32),
            pltpu.VMEM((NG, 128), F32),
            pltpu.VMEM((2, 2, PACKED, 128), F32),
            pltpu.VMEM((2, PACKED, 128), F32),
            pltpu.VMEM((2, PACKED, 128), F32),
            pltpu.VMEM((2, PACKED, 128), F32),
            pltpu.VMEM((3, 2, PACKED, 128), F32),
            dma((2, 3)), dma((2, 3)), dma((2,)), dma((2,)), dma((2,)), dma((2,)), dma((4,)), dma((4,)),
        ],
        compiler_params=pltpu.CompilerParams(
            collective_id=0, has_side_effects=True, vmem_limit_bytes=63 << 20
        ),
        cost_estimate=pl.CostEstimate(flops=10**9, bytes_accessed=4 * 10**6, transcendentals=0),
    )(
        orbitals.reshape(PLANES, cells), sphere_depth,
        jnp.asarray(t1), jnp.asarray(t2), jnp.asarray(t3), jnp.asarray(t3b),
        jnp.asarray(t2b), jnp.asarray(t1b), jnp.asarray(pick),
    )
    return result.reshape(orbitals.shape)


def solution(mesh):
    placed = (P("orb", "fft", None), P())
    return jax.shard_map(
        shards, mesh=mesh, in_specs=placed, out_specs=P("orb", "fft", None), check_vma=False
    )
```

```python
import functools
import math

import jax
import jax.numpy as jnp
import ml_dtypes
import numpy as np
from jax import lax
from jax.experimental import pallas as pl
from jax.experimental.pallas import tpu as pltpu
from jax.sharding import PartitionSpec as P

NG = 96
PLANES = 24
HALF = 24
ROWS = 48
CROP = 23
UNROLL = dict(spread=4, gather=4, forward_y=4, backward_x=2, backward_y=4)
COULOMB = 0.1
BF = jnp.bfloat16
F32 = jnp.float32
MESH = pl.DeviceIdType.MESH


def signed_order(count):
    place = np.arange(count)
    size = (place + 1) // 2
    return np.where(place % 2 == 1, size, -size)


def angle(a, b):
    return 2.0 * math.pi / NG * (np.outer(a, b) % NG)


def half_of(ky):
    return int(ky % 4 in (1, 2))


def pack_blocks():
    place, most = {}, 0
    for half in range(2):
        filled = 0
        for ky in range(HALF):
            for m in range(ROWS // 8):
                left = CROP**2 - ky**2 - (4 * m) ** 2
                if half_of(ky) != half or left < 0:
                    continue
                width = 2 * math.isqrt(left) + 1
                tile, start = divmod(filled, 64)
                end = start + width
                place[ky, m] = [(half, tile, start, start, min(end, 64))]
                if end > 64:
                    place[ky, m].append((half, tile + 1, start + 64, 0, end - 64))
                filled += width
        most = max(most, -(-filled // 64))
    return place, most


PLACE, TILES = pack_blocks()
PACKED = TILES * 8
CUT = TILES // 2 * 8
OWN_CROSS = "early"
SECOND = ("c", "c", "d")
SPREAD_FIRST = True


def split_table(table):
    high = table.astype(ml_dtypes.bfloat16)
    low = (table - high.astype(np.float64)).astype(ml_dtypes.bfloat16)
    return high, low


def make_tables():
    grid = np.arange(NG)
    ky = np.arange(HALF)
    a = angle(ky, grid)
    hi, lo = split_table(np.concatenate([np.cos(a), -np.sin(a)], 0))
    t1 = np.block([[hi, hi], [lo, lo]])

    kx = signed_order(47)
    a = np.zeros((128, 64))
    c, s = np.zeros((128, 64)), np.zeros((128, 64))
    c[:NG, :47] = np.cos(angle(grid, kx))
    s[:NG, :47] = np.sin(angle(grid, kx))
    hi, lo = split_table(np.block([[c, -s], [s, c]]))
    t2 = np.concatenate([hi, lo], 1)
    hi, lo = split_table(np.block([[c.T, s.T], [-s.T, c.T]]))
    t2b = np.concatenate([hi, hi, lo], 0)

    weight = np.where(ky == 0, 1.0, 2.0) / float(NG**3)
    a = angle(grid, ky)
    hi, lo = split_table(np.concatenate([np.cos(a) * weight, -np.sin(a) * weight], 1))
    t1b = np.concatenate([hi, hi, lo], 1)

    kz = signed_order(ROWS)
    t3, t3b = [], []
    for slab in range(NG // PLANES):
        z = slab * PLANES + np.arange(PLANES)
        a = angle(kz, z)
        hi, lo = split_table(np.concatenate([np.cos(a), np.sin(a)], 0))
        t3.append(np.concatenate([hi, hi, lo, lo], 1))
        a = angle(z, kz)
        hi, lo = split_table(np.concatenate([np.cos(a), np.sin(a)], 0))
        t3b.append(np.concatenate([hi, hi, lo], 1))
    pick = np.zeros((HALF, 128), np.float32)
    for lane in range(128):
        if lane % 64 < 47:
            pick[abs(kx[lane % 64]), lane] = 1.0
    return t1, t2, np.stack(t3), np.stack(t3b), t2b, t1b, pick


def lanes(rows):
    return lax.broadcasted_iota(jnp.int32, (rows, 128), 1)


def split(value):
    high = value.astype(BF)
    return high, (value - high.astype(F32)).astype(BF)


def dot(a, b):
    return jnp.dot(a, b, preferred_element_type=F32)


def spread(raw, grid, tile):
    row = tile * 8
    lane = lanes(8)

    @pl.loop(0, NG // 4, unroll=UNROLL["spread"])
    def _(group):
        start = tile * 576 + pl.multiple_of(group * 24, 24)
        t0, t1, t2 = [raw[pl.ds(start + 8 * k, 8), :] for k in range(3)]
        pieces = (
            t0,
            pltpu.roll(jnp.where(lane >= 96, t0, t1), 32, 1),
            pltpu.roll(jnp.where(lane >= 64, t1, t2), 64, 1),
            pltpu.roll(t2, 96, 1),
        )
        for j, piece in enumerate(pieces):
            grid[pl.ds(row * NG + group * 4 + j, 8, stride=NG), :] = piece


def gather(grid, out, tile):
    lane = lanes(8)

    @pl.loop(0, NG // 4, unroll=UNROLL["gather"])
    def _(group):
        a = [grid[pl.ds(tile * 8 * NG + group * 4 + j, 8, stride=NG), :] for j in range(4)]
        r1, r2, r3 = pltpu.roll(a[1], 96, 1), pltpu.roll(a[2], 64, 1), pltpu.roll(a[3], 32, 1)
        start = tile * 576 + pl.multiple_of(group * 24, 24)
        out[pl.ds(start, 8), :] = jnp.where(lane < 96, a[0], r1)
        out[pl.ds(start + 8, 8), :] = jnp.where(lane < 64, r1, r2)
        out[pl.ds(start + 16, 8), :] = jnp.where(lane < 32, r2, r3)


def forward_y(left, right, t1, u, tile):
    @pl.loop(tile * 4, tile * 4 + 4, unroll=UNROLL["forward_y"])
    def _(pair):
        rows = pl.ds(pl.multiple_of(pair * 2 * NG, 2 * NG), 2 * NG)
        hi, lo = split(left[rows, :] * right[rows, :])
        stacked = jnp.concatenate(
            [
                jnp.concatenate([hi[:NG], hi[NG:]], 1),
                jnp.concatenate([lo[:NG], lo[NG:]], 1),
            ],
            0,
        )
        o = dot(t1[...], stacked)
        o = o[:48] + o[48:]
        for t in range(2):
            where = pl.ds(pair * 2 + t, HALF, stride=PLANES)
            u.at[0][where, :] = o[:24, 128 * t : 128 * t + 128]
            u.at[1][where, :] = o[24:, 128 * t : 128 * t + 128]


def forward_x(u, t2, f, tile):
    places = [pl.ds(ky * PLANES + tile * 8, 8) for ky in range(HALF)]
    parts = [jnp.concatenate([u[c, where, :] for where in places], 0) for c in range(2)]
    hi, lo = split(jnp.concatenate(parts, 1))
    o = dot(hi, t2[...])
    o = o[:, :128] + o[:, 128:] + dot(lo, t2[:, :128])
    for ky, where in enumerate(places):
        f[where, :] = o[8 * ky : 8 * ky + 8]


def forward_z(f, t3, coulomb, spectrum):
    sign = jnp.where(lanes(ROWS) < 64, 1.0, -1.0)
    lane = lanes(8) % 64
    written = set()
    for pair in range(HALF // 2):
        v = f[pl.ds(pair * 48, 48), :]
        v = jnp.concatenate([v[:24], v[24:]], 1)
        hi = v.astype(BF).astype(F32)
        lo = v - hi
        o = dot(t3[...], jnp.concatenate([hi, lo, hi, lo], 0).astype(BF))
        for t in range(2):
            ky = pair * 2 + t
            part = o[:, 128 * t : 128 * t + 128]
            part = part[:48] + sign * pltpu.roll(part[48:], 64, 1)
            part = part * coulomb[pl.ds(ky * ROWS, ROWS), :]
            for m in range(ROWS // 8):
                if (ky, m) not in PLACE:
                    continue
                for half, tile, shift, low, high in PLACE[ky, m]:
                    block = part[8 * m : 8 * m + 8]
                    if shift:
                        block = pltpu.roll(block, shift, 1)
                    if len(PLACE[ky, m]) > 1:
                        block = jnp.where((lane >= low) & (lane < high), block, 0.0)
                    rows = pl.ds(tile * 8, 8)
                    if (half, tile) in written:
                        block = block + spectrum[half, rows, :]
                    spectrum[half, rows, :] = block
                    written.add((half, tile))
    for half in range(2):
        for tile in range(TILES):
            if (half, tile) not in written:
                spectrum[half, pl.ds(tile * 8, 8), :] = jnp.zeros((8, 128), F32)


def backward_z(spectrum, t3b, f):
    sign = jnp.where(lanes(PLANES) < 64, -1.0, 1.0)
    lane = lanes(8) % 64
    none = jnp.zeros((8, 128), F32)

    def unpacked(ky):
        blocks = []
        for m in range(ROWS // 8):
            if (ky, m) not in PLACE:
                blocks.append(none)
                continue
            total = None
            for half, tile, shift, low, high in PLACE[ky, m]:
                block = jnp.where((lane >= low) & (lane < high), spectrum[half, pl.ds(tile * 8, 8), :], 0.0)
                if shift:
                    block = pltpu.roll(block, 128 - shift, 1)
                total = block if total is None else total + block
            blocks.append(total)
        return jnp.concatenate(blocks, 0)

    for pair in range(HALF // 2):
        hi, lo = split(jnp.concatenate([unpacked(pair * 2), unpacked(pair * 2 + 1)], 1))
        o = dot(t3b[...], jnp.concatenate([hi, lo, hi], 0))
        for t in range(2):
            part = o[:, 128 * t : 128 * t + 128]
            f[pl.ds(pair * 48 + 24 * t, 24), :] = part[:24] + sign * pltpu.roll(part[24:], 64, 1)


def backward_x(f, t2b, u):
    @pl.loop(0, 4, unroll=UNROLL["backward_x"])
    def _(block):
        rows = pl.ds(pl.multiple_of(block * 144, 144), 144)
        hi, lo = split(f[rows, :])
        o = dot(jnp.concatenate([hi, lo], 1), t2b[:256, :]) + dot(hi, t2b[256:, :])
        u[0, rows, :] = o[:, :128]
        u[1, rows, :] = o[:, 128:]


def backward_y(fields, t1b, orbitals, total, fresh, tile):
    @pl.loop(tile * 4, tile * 4 + 4, unroll=UNROLL["backward_y"])
    def _(pair):
        terms = [None, None]
        for u, orbital in zip(fields, orbitals):
            parts = []
            for t in range(2):
                where = pl.ds(pair * 2 + t, HALF, stride=PLANES)
                parts.append(jnp.concatenate([u.at[0][where, :], u.at[1][where, :]], 0))
            hi, lo = split(jnp.concatenate(parts, 1))
            v = dot(t1b[...], jnp.concatenate([hi, lo, hi], 0))
            for t in range(2):
                rows = pl.ds(pl.multiple_of((pair * 2 + t) * NG, NG), NG)
                term = orbital[rows, :] * v[:, 128 * t : 128 * t + 128]
                terms[t] = term if terms[t] is None else terms[t] + term
        for t in range(2):
            rows = pl.ds(pl.multiple_of((pair * 2 + t) * NG, NG), NG)
            total[rows, :] = terms[t] if fresh else total[rows, :] + terms[t]


def fill_coulomb(depth, pick, coulomb, limits):
    kept = depth[...].astype(F32)[:HALF] + 1.0
    limits[...] = lax.dot_general(
        kept, pick[...], (((0,), (0,)), ((), ())), preferred_element_type=F32
    ) - 1.0
    lane = lax.broadcasted_iota(jnp.int32, (ROWS, 128), 1) % 64
    row = lax.broadcasted_iota(jnp.int32, (ROWS, 128), 0)
    kx, kz = (lane + 1) // 2, (row + 1) // 2
    square = (kx * kx + kz * kz).astype(F32)
    size = kz.astype(F32)

    @pl.loop(0, HALF, unroll=4)
    def _(ky):
        whole = square + (ky * ky).astype(F32)
        inside = (size <= limits[pl.ds(ky, 1), :]) & (whole > 0.5)
        coulomb[pl.ds(pl.multiple_of(ky * ROWS, ROWS), ROWS), :] = jnp.where(
            inside, COULOMB * NG**1.5 / jnp.maximum(whole, 1.0), 0.0
        )


def kernel(
    own_hbm, depth_hbm, t1_hbm, t2_hbm, t3_hbm, t3b_hbm, t2b_hbm, t1b_hbm, pick_hbm, out,
    own, depth, t1, t2, t3, t3b, t2b, t1b, pick, load_sem, raw, grids, total, u, u2, f, coulomb, limits,
    spectra, arrived, summed, crossed, fields,
    phi_send, phi_recv, half_send, half_recv, far_send, far_recv, give_send, give_recv,
):
    orb, fft = lax.axis_index("orb"), lax.axis_index("fft")
    blocks = lax.axis_size("orb")
    core = fft % 2
    other = fft + 1 - 2 * core
    far = (fft + 2) % 4
    near = (orb + blocks - 1 + 2 * core) % blocks
    back = (orb + 1 - 2 * core) % blocks

    loads = [
        pltpu.make_async_copy(src, dst, load_sem.at[place])
        for place, (src, dst) in enumerate((
            (own_hbm, own), (depth_hbm, depth), (pick_hbm, pick), (t1_hbm, t1), (t2_hbm, t2),
            (t3_hbm.at[fft], t3), (t3b_hbm.at[fft], t3b), (t2b_hbm, t2b), (t1b_hbm, t1b),
        ))
    ]
    for load in loads:
        load.start()

    barrier = pltpu.get_barrier_semaphore()
    for peer in ((near, fft), (back, fft), (orb, other), (near, other), (orb, far)):
        pl.semaphore_signal(barrier, inc=1, device_id=peer, device_id_type=MESH)
    pl.semaphore_wait(barrier, 5)

    def send(src, dst, send_sem, recv_sem, peer):
        return pltpu.make_async_remote_copy(
            src_ref=src, dst_ref=dst, send_sem=send_sem, recv_sem=recv_sem,
            device_id=peer, device_id_type=MESH,
        )

    def orbital_copy(phase, tile, peer):
        rows = pl.ds(tile * 576, 576)
        return send(own_hbm.at[rows], raw.at[phase, rows], phi_send.at[phase, tile],
                    phi_recv.at[phase, tile], peer)

    first = [orbital_copy(0, tile, (back, fft)) for tile in range(3)]
    second = [orbital_copy(1, tile, (near, fft)) for tile in range(3)]
    def follow(when):
        for tile in range(3):
            if SECOND[tile] == when:
                second[tile].start()

    for copy in first:
        copy.start()
    follow("a")

    mine, mate, after = grids.at[0], grids.at[1], grids.at[2]
    chunks = [(0, pl.ds(0, PACKED)), (1, pl.ds(0, CUT)), (1, pl.ds(CUT, PACKED - CUT))]
    peers = [(orb, other), (near, other), (near, other)]
    halves = [
        send(spectra.at[pair, 1 - core, rows], arrived.at[pair, rows],
             half_send.at[place], half_recv.at[place], peers[place])
        for place, (pair, rows) in enumerate(chunks)
    ]
    fars = [
        send(summed.at[pair, rows], crossed.at[pair, rows],
             far_send.at[place], far_recv.at[place], (orb, far))
        for place, (pair, rows) in enumerate(chunks)
    ]

    def give(place, slot, field, half, peer):
        pair, rows = chunks[place]
        return send(fields.at[pair, half, rows], fields.at[field, half, rows],
                    give_send.at[place, slot], give_recv.at[place, slot], peer)

    gives = [[give(0, 0, 0, core, (orb, other))]]
    for place in (1, 2):
        gives.append([give(place, 0, 1, core, (near, other)), give(place, 1, 2, core, (orb, other)),
                      give(place, 2, 2, 1 - core, (orb, other))])

    def cross(place):
        pair, rows = chunks[place]
        halves[place].wait_recv()
        summed[pair, rows] = spectra[pair, core, rows] + arrived[pair, rows]
        fars[place].start()

    def hand_out(place):
        pair, rows = chunks[place]
        fars[place].wait_recv()
        fields[pair, core, rows] = summed[pair, rows] + crossed[pair, rows]
        for copy in gives[place][:2]:
            copy.start()

    for load in loads:
        load.wait()
    fill_coulomb(depth, pick, coulomb, limits)
    for tile in range(3):
        spread(own, mine, tile)
        forward_y(mine, mine, t1, u, tile)
        forward_x(u, t2, f, tile)
    forward_z(f, t3, coulomb, spectra.at[0])
    halves[0].start()
    if OWN_CROSS == "early":
        cross(0)

    for tile in range(3):
        first[tile].wait_recv()
        if tile == 2:
            if OWN_CROSS == "arrived":
                cross(0)
            follow("b")
        spread(raw.at[0], mate, tile)
        forward_y(mine, mate, t1, u, tile)
        forward_x(u, t2, f, tile)
    forward_z(f, t3, coulomb, spectra.at[1])
    halves[1].start()
    halves[2].start()
    follow("c")
    if OWN_CROSS == "sent":
        cross(0)
    cross(1)
    cross(2)
    if OWN_CROSS == "last":
        cross(0)
    follow("d")

    hand_out(0)
    gives[0][0].wait_recv()
    backward_z(fields.at[0], t3b, f)
    backward_x(f, t2b, u)
    for tile in range(3):
        backward_y((u,), t1b, (mine,), total, True, tile)

    hand_out(1)
    follow("e")
    hand_out(2)
    follow("f")
    if SPREAD_FIRST:
        for tile in range(3):
            second[tile].wait_recv()
            spread(raw.at[1], after, tile)
    for place in (1, 2):
        gives[place][0].wait_recv()
        gives[place][2].start()
    backward_z(fields.at[1], t3b, f)
    backward_x(f, t2b, u)
    for place in (1, 2):
        gives[place][1].wait_recv()
        gives[place][2].wait_recv()
    backward_z(fields.at[2], t3b, f)
    backward_x(f, t2b, u2)
    for tile in range(3):
        if not SPREAD_FIRST:
            second[tile].wait_recv()
            spread(raw.at[1], after, tile)
        backward_y((u, u2), t1b, (mate, after), total, False, tile)
        gather(total, out, tile)
    for copy in first + second + halves + fars + sum(gives, []):
        copy.wait_send()


def shards(orbitals, sphere_depth):
    t1, t2, t3, t3b, t2b, t1b, pick = make_tables()
    vmem = pl.BlockSpec(memory_space=pltpu.VMEM)
    cells = PLANES * NG * NG // 128
    dma = pltpu.SemaphoreType.DMA
    tiled = orbitals.reshape(PLANES // 8, 8, NG * NG // 128, 128).transpose(0, 2, 1, 3).reshape(cells, 128)
    result = pl.pallas_call(
        kernel,
        out_shape=pltpu.VMEM((cells, 128), F32),
        in_specs=[pl.BlockSpec(memory_space=pltpu.HBM)] * 9,
        out_specs=vmem,
        scratch_shapes=[
            pltpu.VMEM((cells, 128), F32),
            pltpu.VMEM(sphere_depth.shape, jnp.int32),
            pltpu.VMEM(t1.shape, BF),
            pltpu.VMEM(t2.shape, BF),
            pltpu.VMEM(t3.shape[1:], BF),
            pltpu.VMEM(t3b.shape[1:], BF),
            pltpu.VMEM(t2b.shape, BF),
            pltpu.VMEM(t1b.shape, BF),
            pltpu.VMEM(pick.shape, F32),
            dma((9,)),
            pltpu.VMEM((2, cells, 128), F32),
            pltpu.VMEM((3, PLANES * NG, 128), F32),
            pltpu.VMEM((PLANES * NG, 128), F32),
            pltpu.VMEM((2, HALF * PLANES, 128), F32),
            pltpu.VMEM((2, HALF * PLANES, 128), F32),
            pltpu.VMEM((HALF * PLANES, 128), F32),
            pltpu.VMEM((HALF * ROWS, 128), F32),
            pltpu.VMEM((NG, 128), F32),
            pltpu.VMEM((2, 2, PACKED, 128), F32),
            pltpu.VMEM((2, PACKED, 128), F32),
            pltpu.VMEM((2, PACKED, 128), F32),
            pltpu.VMEM((2, PACKED, 128), F32),
            pltpu.VMEM((3, 2, PACKED, 128), F32),
            dma((2, 3)), dma((2, 3)), dma((3,)), dma((3,)), dma((3,)), dma((3,)), dma((3, 3)), dma((3, 3)),
        ],
        compiler_params=pltpu.CompilerParams(
            collective_id=0, has_side_effects=True, vmem_limit_bytes=60 << 20
        ),
        cost_estimate=pl.CostEstimate(flops=10**9, bytes_accessed=4 * 10**6, transcendentals=0),
    )(
        tiled, sphere_depth,
        jnp.asarray(t1), jnp.asarray(t2), jnp.asarray(t3), jnp.asarray(t3b),
        jnp.asarray(t2b), jnp.asarray(t1b), jnp.asarray(pick),
    )
    result = result.reshape(PLANES // 8, NG * NG // 128, 8, 128)
    return result.transpose(0, 2, 1, 3).reshape(orbitals.shape)


def solution(mesh):
    placed = (P("orb", "fft", None), P())
    return jax.shard_map(
        shards, mesh=mesh, in_specs=placed, out_specs=P("orb", "fft", None), check_vma=False
    )
```

```python
import functools
import math

import jax
import jax.numpy as jnp
import ml_dtypes
import numpy as np
from jax import lax
from jax.experimental import pallas as pl
from jax.experimental.pallas import tpu as pltpu
from jax.sharding import PartitionSpec as P

NG = 96
PLANES = 24
HALF = 24
PITCH = 104
ROWS = 48
CROP = 23
UNROLL = dict(spread=4, gather=4, forward_y=4, backward_x=2, backward_y=4)
COULOMB = 0.1
BF = jnp.bfloat16
F32 = jnp.float32
MESH = pl.DeviceIdType.MESH


def signed_order(count):
    place = np.arange(count)
    size = (place + 1) // 2
    return np.where(place % 2 == 1, size, -size)


def angle(a, b):
    return 2.0 * math.pi / NG * (np.outer(a, b) % NG)


def half_of(ky):
    return int(ky % 4 in (1, 2))


def pack_blocks():
    place, most = {}, 0
    for half in range(2):
        filled = 0
        for ky in range(HALF):
            for m in range(ROWS // 8):
                left = CROP**2 - ky**2 - (4 * m) ** 2
                if half_of(ky) != half or left < 0:
                    continue
                width = 2 * math.isqrt(left) + 1
                tile, start = divmod(filled, 64)
                end = start + width
                place[ky, m] = [(half, tile, start, start, min(end, 64))]
                if end > 64:
                    place[ky, m].append((half, tile + 1, start + 64, 0, end - 64))
                filled += width
        most = max(most, -(-filled // 64))
    return place, most


PLACE, TILES = pack_blocks()
PACKED = TILES * 8
CUT = TILES // 2 * 8
OWN_CROSS = "early"
SECOND = ("c", "c", "c")
SPREAD = "first"
ASIDE = (0, 1, 2)
PASS_OWN = "crossed"
PASS_LAST = "crossed"


def split_table(table):
    high = table.astype(ml_dtypes.bfloat16)
    low = (table - high.astype(np.float64)).astype(ml_dtypes.bfloat16)
    return high, low


def make_tables():
    grid = np.arange(NG)
    ky = np.arange(HALF)
    a = angle(ky, grid)
    hi, lo = split_table(np.concatenate([np.cos(a), -np.sin(a)], 0))
    t1 = np.block([[hi, hi], [lo, lo]])

    kx = signed_order(47)
    a = np.zeros((128, 64))
    c, s = np.zeros((128, 64)), np.zeros((128, 64))
    c[:NG, :47] = np.cos(angle(grid, kx))
    s[:NG, :47] = np.sin(angle(grid, kx))
    hi, lo = split_table(np.block([[c, -s], [s, c]]))
    t2 = np.concatenate([hi, lo], 1)
    hi, lo = split_table(np.block([[c.T, s.T], [-s.T, c.T]]))
    t2b = np.concatenate([hi, hi, lo], 0)

    weight = np.where(ky == 0, 1.0, 2.0) / float(NG**3)
    a = angle(grid, ky)
    hi, lo = split_table(np.concatenate([np.cos(a) * weight, -np.sin(a) * weight], 1))
    t1b = np.concatenate([hi, hi, lo], 1)

    kz = signed_order(ROWS)
    t3, t3b = [], []
    for slab in range(NG // PLANES):
        z = slab * PLANES + np.arange(PLANES)
        a = angle(kz, z)
        hi, lo = split_table(np.concatenate([np.cos(a), np.sin(a)], 0))
        t3.append(np.concatenate([hi, hi, lo, lo], 1))
        a = angle(z, kz)
        hi, lo = split_table(np.concatenate([np.cos(a), np.sin(a)], 0))
        t3b.append(np.concatenate([hi, hi, lo], 1))
    pick = np.zeros((HALF, 128), np.float32)
    for lane in range(128):
        if lane % 64 < 47:
            pick[abs(kx[lane % 64]), lane] = 1.0
    return t1, t2, np.stack(t3), np.stack(t3b), t2b, t1b, pick


def lanes(rows):
    return lax.broadcasted_iota(jnp.int32, (rows, 128), 1)


def split(value):
    high = value.astype(BF)
    return high, (value - high.astype(F32)).astype(BF)


def dot(a, b):
    return jnp.dot(a, b, preferred_element_type=F32)


def spread(raw, grid, tile):
    row = tile * 8
    lane = lanes(8)

    @pl.loop(0, NG // 4, unroll=UNROLL["spread"])
    def _(group):
        start = tile * 576 + pl.multiple_of(group * 24, 24)
        t0, t1, t2 = [raw[pl.ds(start + 8 * k, 8), :] for k in range(3)]
        pieces = (
            t0,
            pltpu.roll(jnp.where(lane >= 96, t0, t1), 32, 1),
            pltpu.roll(jnp.where(lane >= 64, t1, t2), 64, 1),
            pltpu.roll(t2, 96, 1),
        )
        for j, piece in enumerate(pieces):
            grid[pl.ds(row * PITCH + group * 4 + j, 8, stride=PITCH), :] = piece


def gather(grid, out, tile):
    lane = lanes(8)

    @pl.loop(0, NG // 4, unroll=UNROLL["gather"])
    def _(group):
        a = [grid[pl.ds(tile * 8 * PITCH + group * 4 + j, 8, stride=PITCH), :] for j in range(4)]
        r1, r2, r3 = pltpu.roll(a[1], 96, 1), pltpu.roll(a[2], 64, 1), pltpu.roll(a[3], 32, 1)
        start = tile * 576 + pl.multiple_of(group * 24, 24)
        out[pl.ds(start, 8), :] = jnp.where(lane < 96, a[0], r1)
        out[pl.ds(start + 8, 8), :] = jnp.where(lane < 64, r1, r2)
        out[pl.ds(start + 16, 8), :] = jnp.where(lane < 32, r2, r3)


def forward_y(left, right, t1, u, tile):
    @pl.loop(tile * 4, tile * 4 + 4, unroll=UNROLL["forward_y"])
    def _(pair):
        planes = [pl.ds(pl.multiple_of((pair * 2 + t) * PITCH, PITCH), NG) for t in range(2)]
        hi, lo = split(jnp.concatenate([left[rows, :] * right[rows, :] for rows in planes], 1))
        o = dot(t1[...], jnp.concatenate([hi, lo], 0))
        o = o[:48] + o[48:]
        for t in range(2):
            where = pl.ds(pair * 2 + t, HALF, stride=PLANES)
            u.at[0][where, :] = o[:24, 128 * t : 128 * t + 128]
            u.at[1][where, :] = o[24:, 128 * t : 128 * t + 128]


def forward_x(u, t2, f, tile):
    places = [pl.ds(ky * PLANES + tile * 8, 8) for ky in range(HALF)]
    parts = [jnp.concatenate([u[c, where, :] for where in places], 0) for c in range(2)]
    hi, lo = split(jnp.concatenate(parts, 1))
    o = dot(hi, t2[...])
    o = o[:, :128] + o[:, 128:] + dot(lo, t2[:, :128])
    for ky, where in enumerate(places):
        f[where, :] = o[8 * ky : 8 * ky + 8]


def forward_z(f, t3, coulomb, spectrum):
    sign = jnp.where(lanes(ROWS) < 64, 1.0, -1.0)
    lane = lanes(8) % 64
    written = set()
    for pair in range(HALF // 2):
        v = f[pl.ds(pair * 48, 48), :]
        v = jnp.concatenate([v[:24], v[24:]], 1)
        hi = v.astype(BF).astype(F32)
        lo = v - hi
        o = dot(t3[...], jnp.concatenate([hi, lo, hi, lo], 0).astype(BF))
        for t in range(2):
            ky = pair * 2 + t
            part = o[:, 128 * t : 128 * t + 128]
            part = part[:48] + sign * pltpu.roll(part[48:], 64, 1)
            part = part * coulomb[pl.ds(ky * ROWS, ROWS), :]
            for m in range(ROWS // 8):
                if (ky, m) not in PLACE:
                    continue
                for half, tile, shift, low, high in PLACE[ky, m]:
                    block = part[8 * m : 8 * m + 8]
                    if shift:
                        block = pltpu.roll(block, shift, 1)
                    if len(PLACE[ky, m]) > 1:
                        block = jnp.where((lane >= low) & (lane < high), block, 0.0)
                    rows = pl.ds(tile * 8, 8)
                    if (half, tile) in written:
                        block = block + spectrum[half, rows, :]
                    spectrum[half, rows, :] = block
                    written.add((half, tile))
    for half in range(2):
        for tile in range(TILES):
            if (half, tile) not in written:
                spectrum[half, pl.ds(tile * 8, 8), :] = jnp.zeros((8, 128), F32)


def backward_z(spectrum, t3b, f):
    sign = jnp.where(lanes(PLANES) < 64, -1.0, 1.0)
    lane = lanes(8) % 64
    none = jnp.zeros((8, 128), F32)

    def unpacked(ky):
        blocks = []
        for m in range(ROWS // 8):
            if (ky, m) not in PLACE:
                blocks.append(none)
                continue
            total = None
            for half, tile, shift, low, high in PLACE[ky, m]:
                block = jnp.where((lane >= low) & (lane < high), spectrum[half, pl.ds(tile * 8, 8), :], 0.0)
                if shift:
                    block = pltpu.roll(block, 128 - shift, 1)
                total = block if total is None else total + block
            blocks.append(total)
        return jnp.concatenate(blocks, 0)

    for pair in range(HALF // 2):
        hi, lo = split(jnp.concatenate([unpacked(pair * 2), unpacked(pair * 2 + 1)], 1))
        o = dot(t3b[...], jnp.concatenate([hi, lo, hi], 0))
        for t in range(2):
            part = o[:, 128 * t : 128 * t + 128]
            f[pl.ds(pair * 48 + 24 * t, 24), :] = part[:24] + sign * pltpu.roll(part[24:], 64, 1)


def backward_x(f, t2b, u):
    @pl.loop(0, 4, unroll=UNROLL["backward_x"])
    def _(block):
        rows = pl.ds(pl.multiple_of(block * 144, 144), 144)
        hi, lo = split(f[rows, :])
        o = dot(jnp.concatenate([hi, lo], 1), t2b[:256, :]) + dot(hi, t2b[256:, :])
        u[0, rows, :] = o[:, :128]
        u[1, rows, :] = o[:, 128:]


def backward_y(fields, t1b, orbitals, total, fresh, tile):
    @pl.loop(tile * 4, tile * 4 + 4, unroll=UNROLL["backward_y"])
    def _(pair):
        terms = [None, None]
        for u, orbital in zip(fields, orbitals):
            parts = []
            for t in range(2):
                where = pl.ds(pair * 2 + t, HALF, stride=PLANES)
                parts.append(jnp.concatenate([u.at[0][where, :], u.at[1][where, :]], 0))
            hi, lo = split(jnp.concatenate(parts, 1))
            v = dot(t1b[...], jnp.concatenate([hi, lo, hi], 0))
            for t in range(2):
                rows = pl.ds(pl.multiple_of((pair * 2 + t) * PITCH, PITCH), NG)
                term = orbital[rows, :] * v[:, 128 * t : 128 * t + 128]
                terms[t] = term if terms[t] is None else terms[t] + term
        for t in range(2):
            rows = pl.ds(pl.multiple_of((pair * 2 + t) * PITCH, PITCH), NG)
            total[rows, :] = terms[t] if fresh else total[rows, :] + terms[t]


def fill_coulomb(depth, pick, coulomb, limits):
    kept = depth[...].astype(F32)[:HALF] + 1.0
    limits[...] = lax.dot_general(
        kept, pick[...], (((0,), (0,)), ((), ())), preferred_element_type=F32
    ) - 1.0
    lane = lax.broadcasted_iota(jnp.int32, (ROWS, 128), 1) % 64
    row = lax.broadcasted_iota(jnp.int32, (ROWS, 128), 0)
    kx, kz = (lane + 1) // 2, (row + 1) // 2
    square = (kx * kx + kz * kz).astype(F32)
    size = kz.astype(F32)

    @pl.loop(0, HALF, unroll=4)
    def _(ky):
        whole = square + (ky * ky).astype(F32)
        inside = (size <= limits[pl.ds(ky, 1), :]) & (whole > 0.5)
        coulomb[pl.ds(pl.multiple_of(ky * ROWS, ROWS), ROWS), :] = jnp.where(
            inside, COULOMB * NG**1.5 / jnp.maximum(whole, 1.0), 0.0
        )


def kernel(
    own_hbm, depth_hbm, t1_hbm, t2_hbm, t3_hbm, t3b_hbm, t2b_hbm, t1b_hbm, pick_hbm, out,
    own, depth, t1, t2, t3, t3b, t2b, t1b, pick, load_sem, raw, grids, total, u, u2, f, coulomb, limits,
    spectra, arrived, summed, passing, crossed, fields,
    phi_send, phi_recv, half_send, half_recv, far_send, far_recv, aside_send, aside_recv, give_send, give_recv,
):
    orb, fft = lax.axis_index("orb"), lax.axis_index("fft")
    blocks = lax.axis_size("orb")
    core = fft % 2
    other = fft + 1 - 2 * core
    far = (fft + 2) % 4
    near = (orb + blocks - 1 + 2 * core) % blocks
    back = (orb + 1 - 2 * core) % blocks
    aside = orb + 1 - 2 * (orb % 2)
    inner = (orb % 4 + 1) % 4 >= 2

    loads = [
        pltpu.make_async_copy(src, dst, load_sem.at[place])
        for place, (src, dst) in enumerate((
            (own_hbm, own), (depth_hbm, depth), (pick_hbm, pick), (t1_hbm, t1), (t2_hbm, t2),
            (t3_hbm.at[fft], t3), (t3b_hbm.at[fft], t3b), (t2b_hbm, t2b), (t1b_hbm, t1b),
        ))
    ]
    for load in loads:
        load.start()

    barrier = pltpu.get_barrier_semaphore()
    for peer in ((near, fft), (back, fft), (orb, other), (near, other), (orb, far), (aside, far)):
        pl.semaphore_signal(barrier, inc=1, device_id=peer, device_id_type=MESH)
    pl.semaphore_wait(barrier, 6)

    def send(src, dst, send_sem, recv_sem, peer):
        return pltpu.make_async_remote_copy(
            src_ref=src, dst_ref=dst, send_sem=send_sem, recv_sem=recv_sem,
            device_id=peer, device_id_type=MESH,
        )

    def orbital_copy(phase, tile, peer):
        rows = pl.ds(tile * 576, 576)
        return send(own_hbm.at[rows], raw.at[phase, rows], phi_send.at[phase, tile],
                    phi_recv.at[phase, tile], peer)

    first = [orbital_copy(0, tile, (back, fft)) for tile in range(3)]
    second = [orbital_copy(1, tile, (near, fft)) for tile in range(3)]
    def follow(when):
        for tile in range(3):
            if SECOND[tile] == when:
                second[tile].start()

    for copy in first:
        copy.start()
    follow("a")

    mine, mate, after = grids.at[0], grids.at[1], grids.at[2]
    chunks = [(0, pl.ds(0, PACKED)), (1, pl.ds(0, CUT)), (1, pl.ds(CUT, PACKED - CUT))]
    peers = [(orb, other), (near, other), (near, other)]
    halves = [
        send(spectra.at[pair, 1 - core, rows], arrived.at[pair, rows],
             half_send.at[place], half_recv.at[place], peers[place])
        for place, (pair, rows) in enumerate(chunks)
    ]
    fars = [
        send(summed.at[pair, rows], crossed.at[pair, rows],
             far_send.at[place], far_recv.at[place], (orb, far))
        for place, (pair, rows) in enumerate(chunks)
    ]

    asides = [
        send(summed.at[pair, rows], passing.at[pair, rows],
             aside_send.at[place], aside_recv.at[place], (aside, fft))
        for place, (pair, rows) in enumerate(chunks)
    ]
    onward = [
        send(passing.at[pair, rows], crossed.at[pair, rows],
             aside_send.at[place], far_recv.at[place], (aside, far))
        for place, (pair, rows) in enumerate(chunks)
    ]

    def give(place, slot, field, half, peer):
        pair, rows = chunks[place]
        return send(fields.at[pair, half, rows], fields.at[field, half, rows],
                    give_send.at[place, slot], give_recv.at[place, slot], peer)

    gives = [[give(0, 0, 0, core, (orb, other))]]
    for place in (1, 2):
        gives.append([give(place, 0, 1, core, (near, other)), give(place, 1, 2, core, (orb, other)),
                      give(place, 2, 2, 1 - core, (orb, other))])

    def cross(place):
        pair, rows = chunks[place]
        halves[place].wait_recv()
        summed[pair, rows] = spectra[pair, core, rows] + arrived[pair, rows]
        if place in ASIDE:
            pl.when(inner)(fars[place].start)
            pl.when(jnp.logical_not(inner))(asides[place].start)
        else:
            fars[place].start()

    def pass_on(place):
        if place in ASIDE:
            @pl.when(inner)
            def _():
                asides[place].wait_recv()
                onward[place].start()

    def hand_out(place):
        pair, rows = chunks[place]
        fars[place].wait_recv()
        fields[pair, core, rows] = summed[pair, rows] + crossed[pair, rows]
        for copy in gives[place][:2]:
            copy.start()

    for load in loads:
        load.wait()
    fill_coulomb(depth, pick, coulomb, limits)
    for tile in range(3):
        spread(own, mine, tile)
        forward_y(mine, mine, t1, u, tile)
        forward_x(u, t2, f, tile)
    forward_z(f, t3, coulomb, spectra.at[0])
    halves[0].start()
    if OWN_CROSS == "early":
        cross(0)

    for tile in range(3):
        first[tile].wait_recv()
        if tile == 2:
            if OWN_CROSS == "arrived":
                cross(0)
            follow("b")
        spread(raw.at[0], mate, tile)
        forward_y(mine, mate, t1, u, tile)
        forward_x(u, t2, f, tile)
    forward_z(f, t3, coulomb, spectra.at[1])
    if PASS_OWN == "sent":
        pass_on(0)
    halves[1].start()
    halves[2].start()
    follow("c")
    if OWN_CROSS == "sent":
        cross(0)
    cross(1)
    cross(2)
    if OWN_CROSS == "last":
        cross(0)
    follow("d")
    if PASS_OWN == "crossed":
        pass_on(0)
    pass_on(1)
    if PASS_LAST == "crossed":
        pass_on(2)

    hand_out(0)
    gives[0][0].wait_recv()
    backward_z(fields.at[0], t3b, f)
    backward_x(f, t2b, u)
    for tile in range(3):
        backward_y((u,), t1b, (mine,), total, True, tile)

    if PASS_LAST == "own":
        pass_on(2)
    hand_out(1)
    follow("e")
    hand_out(2)
    follow("f")
    def arrive(when):
        if SPREAD == when:
            for tile in range(3):
                second[tile].wait_recv()
                spread(raw.at[1], after, tile)

    arrive("first")
    for place in (1, 2):
        gives[place][0].wait_recv()
        gives[place][2].start()
    arrive("second")
    backward_z(fields.at[1], t3b, f)
    backward_x(f, t2b, u)
    arrive("third")
    for place in (1, 2):
        gives[place][1].wait_recv()
        gives[place][2].wait_recv()
    backward_z(fields.at[2], t3b, f)
    backward_x(f, t2b, u2)
    arrive("last")
    for tile in range(3):
        backward_y((u, u2), t1b, (mate, after), total, False, tile)
        gather(total, out, tile)
    for copy in first + second + halves + sum(gives, []):
        copy.wait_send()
    for place in range(3):
        if place in ASIDE:
            @pl.when(inner)
            def _():
                fars[place].wait_send()
                onward[place].wait_send()

            pl.when(jnp.logical_not(inner))(asides[place].wait_send)
        else:
            fars[place].wait_send()


def shards(orbitals, sphere_depth):
    t1, t2, t3, t3b, t2b, t1b, pick = make_tables()
    vmem = pl.BlockSpec(memory_space=pltpu.VMEM)
    cells = PLANES * NG * NG // 128
    dma = pltpu.SemaphoreType.DMA
    tiled = orbitals.reshape(PLANES // 8, 8, NG * NG // 128, 128).transpose(0, 2, 1, 3).reshape(cells, 128)
    result = pl.pallas_call(
        kernel,
        out_shape=pltpu.VMEM((cells, 128), F32),
        in_specs=[pl.BlockSpec(memory_space=pltpu.HBM)] * 9,
        out_specs=vmem,
        scratch_shapes=[
            pltpu.VMEM((cells, 128), F32),
            pltpu.VMEM(sphere_depth.shape, jnp.int32),
            pltpu.VMEM(t1.shape, BF),
            pltpu.VMEM(t2.shape, BF),
            pltpu.VMEM(t3.shape[1:], BF),
            pltpu.VMEM(t3b.shape[1:], BF),
            pltpu.VMEM(t2b.shape, BF),
            pltpu.VMEM(t1b.shape, BF),
            pltpu.VMEM(pick.shape, F32),
            dma((9,)),
            pltpu.VMEM((2, cells, 128), F32),
            pltpu.VMEM((3, PLANES * PITCH, 128), F32),
            pltpu.VMEM((PLANES * PITCH, 128), F32),
            pltpu.VMEM((2, HALF * PLANES, 128), F32),
            pltpu.VMEM((2, HALF * PLANES, 128), F32),
            pltpu.VMEM((HALF * PLANES, 128), F32),
            pltpu.VMEM((HALF * ROWS, 128), F32),
            pltpu.VMEM((NG, 128), F32),
            pltpu.VMEM((2, 2, PACKED, 128), F32),
            pltpu.VMEM((2, PACKED, 128), F32),
            pltpu.VMEM((2, PACKED, 128), F32),
            pltpu.VMEM((2, PACKED, 128), F32),
            pltpu.VMEM((2, PACKED, 128), F32),
            pltpu.VMEM((3, 2, PACKED, 128), F32),
            dma((2, 3)), dma((2, 3)), dma((3,)), dma((3,)), dma((3,)), dma((3,)), dma((3,)), dma((3,)), dma((3, 3)), dma((3, 3)),
        ],
        compiler_params=pltpu.CompilerParams(
            collective_id=0, has_side_effects=True, vmem_limit_bytes=60 << 20
        ),
        cost_estimate=pl.CostEstimate(flops=10**9, bytes_accessed=4 * 10**6, transcendentals=0),
    )(
        tiled, sphere_depth,
        jnp.asarray(t1), jnp.asarray(t2), jnp.asarray(t3), jnp.asarray(t3b),
        jnp.asarray(t2b), jnp.asarray(t1b), jnp.asarray(pick),
    )
    result = result.reshape(PLANES // 8, NG * NG // 128, 8, 128)
    return result.transpose(0, 2, 1, 3).reshape(orbitals.shape)


def solution(mesh):
    placed = (P("orb", "fft", None), P())
    return jax.shard_map(
        shards, mesh=mesh, in_specs=placed, out_specs=P("orb", "fft", None), check_vma=False
    )
```

```python
import functools
import math

import jax
import jax.numpy as jnp
import ml_dtypes
import numpy as np
from jax import lax
from jax.experimental import pallas as pl
from jax.experimental.pallas import tpu as pltpu
from jax.sharding import PartitionSpec as P

NG = 96
PLANES = 24
HALF = 24
PITCH = 104
ROWS = 48
CROP = 23
UNROLL = dict(spread=24, gather=24, forward_y=4, backward_x=4, backward_y=4)
COULOMB = 0.1
BF = jnp.bfloat16
F32 = jnp.float32
MESH = pl.DeviceIdType.MESH


def signed_order(count):
    place = np.arange(count)
    size = (place + 1) // 2
    return np.where(place % 2 == 1, size, -size)


def angle(a, b):
    return 2.0 * math.pi / NG * (np.outer(a, b) % NG)


def half_of(ky):
    return int(ky % 4 in (1, 2))


def pack_blocks():
    place, most = {}, 0
    for half in range(2):
        filled = 0
        for ky in range(HALF):
            for m in range(ROWS // 8):
                left = CROP**2 - ky**2 - (4 * m) ** 2
                if half_of(ky) != half or left < 0:
                    continue
                width = 2 * math.isqrt(left) + 1
                tile, start = divmod(filled, 64)
                end = start + width
                place[ky, m] = [(half, tile, start, start, min(end, 64))]
                if end > 64:
                    place[ky, m].append((half, tile + 1, start + 64, 0, end - 64))
                filled += width
        most = max(most, -(-filled // 64))
    return place, most


PLACE, TILES = pack_blocks()
PACKED = TILES * 8
CUT = TILES // 2 * 8
OWN_CROSS = "early"
SECOND = ("c", "c", "c")
SPREAD = "first"
ASIDE = (0, 1, 2)
PASS_OWN = "crossed"
PASS_LAST = "crossed"


def split_table(table):
    high = table.astype(ml_dtypes.bfloat16)
    low = (table - high.astype(np.float64)).astype(ml_dtypes.bfloat16)
    return high, low


def make_tables():
    grid = np.arange(NG)
    ky = np.arange(HALF)
    a = angle(ky, grid)
    hi, lo = split_table(np.concatenate([np.cos(a), -np.sin(a)], 0))
    t1 = np.block([[hi, hi], [lo, lo]])

    kx = signed_order(47)
    a = np.zeros((128, 64))
    c, s = np.zeros((128, 64)), np.zeros((128, 64))
    c[:NG, :47] = np.cos(angle(grid, kx))
    s[:NG, :47] = np.sin(angle(grid, kx))
    hi, lo = split_table(np.block([[c, -s], [s, c]]))
    t2 = np.concatenate([hi, lo], 1)
    hi, lo = split_table(np.block([[c.T, s.T], [-s.T, c.T]]))
    t2b = np.concatenate([hi, hi, lo], 0)

    weight = np.where(ky == 0, 1.0, 2.0) / float(NG**3)
    a = angle(grid, ky)
    hi, lo = split_table(np.concatenate([np.cos(a) * weight, -np.sin(a) * weight], 1))
    t1b = np.concatenate([hi, hi, lo], 1)

    kz = signed_order(ROWS)
    t3, t3b = [], []
    for slab in range(NG // PLANES):
        z = slab * PLANES + np.arange(PLANES)
        a = angle(kz, z)
        hi, lo = split_table(np.concatenate([np.cos(a), np.sin(a)], 0))
        t3.append(np.concatenate([hi, hi, lo, lo], 1))
        a = angle(z, kz)
        hi, lo = split_table(np.concatenate([np.cos(a), np.sin(a)], 0))
        t3b.append(np.concatenate([hi, hi, lo], 1))
    pick = np.zeros((HALF, 128), np.float32)
    for lane in range(128):
        if lane % 64 < 47:
            pick[abs(kx[lane % 64]), lane] = 1.0
    return t1, t2, np.stack(t3), np.stack(t3b), t2b, t1b, pick


def lanes(rows):
    return lax.broadcasted_iota(jnp.int32, (rows, 128), 1)


def split(value):
    high = value.astype(BF)
    return high, (value - high.astype(F32)).astype(BF)


def dot(a, b):
    return jnp.dot(a, b, preferred_element_type=F32)


def spread(raw, grid, tile):
    row = tile * 8
    lane = lanes(8)

    @pl.loop(0, NG // 4, unroll=UNROLL["spread"])
    def _(group):
        start = tile * 576 + pl.multiple_of(group * 24, 24)
        t0, t1, t2 = [raw[pl.ds(start + 8 * k, 8), :] for k in range(3)]
        pieces = (
            t0,
            pltpu.roll(jnp.where(lane >= 96, t0, t1), 32, 1),
            pltpu.roll(jnp.where(lane >= 64, t1, t2), 64, 1),
            pltpu.roll(t2, 96, 1),
        )
        for j, piece in enumerate(pieces):
            grid[pl.ds(row * PITCH + group * 4 + j, 8, stride=PITCH), :] = piece


def gather(grid, out, tile):
    lane = lanes(8)

    @pl.loop(0, NG // 4, unroll=UNROLL["gather"])
    def _(group):
        a = [grid[pl.ds(tile * 8 * PITCH + group * 4 + j, 8, stride=PITCH), :] for j in range(4)]
        r1, r2, r3 = pltpu.roll(a[1], 96, 1), pltpu.roll(a[2], 64, 1), pltpu.roll(a[3], 32, 1)
        start = tile * 576 + pl.multiple_of(group * 24, 24)
        out[pl.ds(start, 8), :] = jnp.where(lane < 96, a[0], r1)
        out[pl.ds(start + 8, 8), :] = jnp.where(lane < 64, r1, r2)
        out[pl.ds(start + 16, 8), :] = jnp.where(lane < 32, r2, r3)


def forward_y(left, right, t1, u, tile):
    @pl.loop(tile * 4, tile * 4 + 4, unroll=UNROLL["forward_y"])
    def _(pair):
        planes = [pl.ds(pl.multiple_of((pair * 2 + t) * PITCH, PITCH), NG) for t in range(2)]
        hi, lo = split(jnp.concatenate([left[rows, :] * right[rows, :] for rows in planes], 1))
        o = dot(t1[...], jnp.concatenate([hi, lo], 0))
        o = o[:48] + o[48:]
        for t in range(2):
            where = pl.ds(pair * 2 + t, HALF, stride=PLANES)
            u.at[0][where, :] = o[:24, 128 * t : 128 * t + 128]
            u.at[1][where, :] = o[24:, 128 * t : 128 * t + 128]


def forward_x(u, t2, f, tile):
    places = [pl.ds(ky * PLANES + tile * 8, 8) for ky in range(HALF)]
    parts = [jnp.concatenate([u[c, where, :] for where in places], 0) for c in range(2)]
    hi, lo = split(jnp.concatenate(parts, 1))
    o = dot(hi, t2[...])
    o = o[:, :128] + o[:, 128:] + dot(lo, t2[:, :128])
    for ky, where in enumerate(places):
        f[where, :] = o[8 * ky : 8 * ky + 8]


def forward_z(f, t3, coulomb, spectrum):
    sign = jnp.where(lanes(ROWS) < 64, 1.0, -1.0)
    lane = lanes(8) % 64
    written = set()
    for pair in range(HALF // 2):
        v = f[pl.ds(pair * 48, 48), :]
        v = jnp.concatenate([v[:24], v[24:]], 1)
        hi = v.astype(BF).astype(F32)
        lo = v - hi
        o = dot(t3[...], jnp.concatenate([hi, lo, hi, lo], 0).astype(BF))
        for t in range(2):
            ky = pair * 2 + t
            part = o[:, 128 * t : 128 * t + 128]
            part = part[:48] + sign * pltpu.roll(part[48:], 64, 1)
            part = part * coulomb[pl.ds(ky * ROWS, ROWS), :]
            for m in range(ROWS // 8):
                if (ky, m) not in PLACE:
                    continue
                for half, tile, shift, low, high in PLACE[ky, m]:
                    block = part[8 * m : 8 * m + 8]
                    if shift:
                        block = pltpu.roll(block, shift, 1)
                    if len(PLACE[ky, m]) > 1:
                        block = jnp.where((lane >= low) & (lane < high), block, 0.0)
                    rows = pl.ds(tile * 8, 8)
                    if (half, tile) in written:
                        block = block + spectrum[half, rows, :]
                    spectrum[half, rows, :] = block
                    written.add((half, tile))
    for half in range(2):
        for tile in range(TILES):
            if (half, tile) not in written:
                spectrum[half, pl.ds(tile * 8, 8), :] = jnp.zeros((8, 128), F32)


def backward_z(spectrum, t3b, f):
    sign = jnp.where(lanes(PLANES) < 64, -1.0, 1.0)
    lane = lanes(8) % 64
    none = jnp.zeros((8, 128), F32)

    def unpacked(ky):
        blocks = []
        for m in range(ROWS // 8):
            if (ky, m) not in PLACE:
                blocks.append(none)
                continue
            total = None
            for half, tile, shift, low, high in PLACE[ky, m]:
                block = jnp.where((lane >= low) & (lane < high), spectrum[half, pl.ds(tile * 8, 8), :], 0.0)
                if shift:
                    block = pltpu.roll(block, 128 - shift, 1)
                total = block if total is None else total + block
            blocks.append(total)
        return jnp.concatenate(blocks, 0)

    for pair in range(HALF // 2):
        hi, lo = split(jnp.concatenate([unpacked(pair * 2), unpacked(pair * 2 + 1)], 1))
        o = dot(t3b[...], jnp.concatenate([hi, lo, hi], 0))
        for t in range(2):
            part = o[:, 128 * t : 128 * t + 128]
            f[pl.ds(pair * 48 + 24 * t, 24), :] = part[:24] + sign * pltpu.roll(part[24:], 64, 1)


def backward_x(f, t2b, u):
    @pl.loop(0, 4, unroll=UNROLL["backward_x"])
    def _(block):
        rows = pl.ds(pl.multiple_of(block * 144, 144), 144)
        hi, lo = split(f[rows, :])
        o = dot(jnp.concatenate([hi, lo], 1), t2b[:256, :]) + dot(hi, t2b[256:, :])
        u[0, rows, :] = o[:, :128]
        u[1, rows, :] = o[:, 128:]


def backward_y(fields, t1b, orbitals, total, fresh, tile):
    @pl.loop(tile * 4, tile * 4 + 4, unroll=UNROLL["backward_y"])
    def _(pair):
        terms = [None, None]
        for u, orbital in zip(fields, orbitals):
            parts = []
            for t in range(2):
                where = pl.ds(pair * 2 + t, HALF, stride=PLANES)
                parts.append(jnp.concatenate([u.at[0][where, :], u.at[1][where, :]], 0))
            hi, lo = split(jnp.concatenate(parts, 1))
            v = dot(t1b[...], jnp.concatenate([hi, lo, hi], 0))
            for t in range(2):
                rows = pl.ds(pl.multiple_of((pair * 2 + t) * PITCH, PITCH), NG)
                term = orbital[rows, :] * v[:, 128 * t : 128 * t + 128]
                terms[t] = term if terms[t] is None else terms[t] + term
        for t in range(2):
            rows = pl.ds(pl.multiple_of((pair * 2 + t) * PITCH, PITCH), NG)
            total[rows, :] = terms[t] if fresh else total[rows, :] + terms[t]


def fill_coulomb(depth, pick, coulomb, limits):
    kept = depth[...].astype(F32)[:HALF] + 1.0
    limits[...] = lax.dot_general(
        kept, pick[...], (((0,), (0,)), ((), ())), preferred_element_type=F32
    ) - 1.0
    lane = lax.broadcasted_iota(jnp.int32, (ROWS, 128), 1) % 64
    row = lax.broadcasted_iota(jnp.int32, (ROWS, 128), 0)
    kx, kz = (lane + 1) // 2, (row + 1) // 2
    square = (kx * kx + kz * kz).astype(F32)
    size = kz.astype(F32)

    @pl.loop(0, HALF, unroll=4)
    def _(ky):
        whole = square + (ky * ky).astype(F32)
        inside = (size <= limits[pl.ds(ky, 1), :]) & (whole > 0.5)
        coulomb[pl.ds(pl.multiple_of(ky * ROWS, ROWS), ROWS), :] = jnp.where(
            inside, COULOMB * NG**1.5 / jnp.maximum(whole, 1.0), 0.0
        )


def kernel(
    own_hbm, depth_hbm, t1_hbm, t2_hbm, t3_hbm, t3b_hbm, t2b_hbm, t1b_hbm, pick_hbm, out,
    own, depth, t1, t2, t3, t3b, t2b, t1b, pick, load_sem, raw, grids, total, u, u2, f, coulomb, limits,
    spectra, arrived, summed, passing, crossed, fields,
    phi_send, phi_recv, half_send, half_recv, far_send, far_recv, aside_send, aside_recv, give_send, give_recv,
):
    orb, fft = lax.axis_index("orb"), lax.axis_index("fft")
    blocks = lax.axis_size("orb")
    core = fft % 2
    other = fft + 1 - 2 * core
    far = (fft + 2) % 4
    near = (orb + blocks - 1 + 2 * core) % blocks
    back = (orb + 1 - 2 * core) % blocks
    aside = orb + 1 - 2 * (orb % 2)
    inner = (orb % 4 + 1) % 4 >= 2

    loads = [
        pltpu.make_async_copy(src, dst, load_sem.at[place])
        for place, (src, dst) in enumerate((
            (own_hbm, own), (depth_hbm, depth), (pick_hbm, pick), (t1_hbm, t1), (t2_hbm, t2),
            (t3_hbm.at[fft], t3), (t3b_hbm.at[fft], t3b), (t2b_hbm, t2b), (t1b_hbm, t1b),
        ))
    ]
    for load in loads:
        load.start()

    barrier = pltpu.get_barrier_semaphore()
    for peer in ((near, fft), (back, fft), (orb, other), (near, other), (orb, far), (aside, far)):
        pl.semaphore_signal(barrier, inc=1, device_id=peer, device_id_type=MESH)
    pl.semaphore_wait(barrier, 6)

    def send(src, dst, send_sem, recv_sem, peer):
        return pltpu.make_async_remote_copy(
            src_ref=src, dst_ref=dst, send_sem=send_sem, recv_sem=recv_sem,
            device_id=peer, device_id_type=MESH,
        )

    def orbital_copy(phase, tile, peer):
        rows = pl.ds(tile * 576, 576)
        return send(own_hbm.at[rows], raw.at[phase, rows], phi_send.at[phase, tile],
                    phi_recv.at[phase, tile], peer)

    first = [orbital_copy(0, tile, (back, fft)) for tile in range(3)]
    second = [orbital_copy(1, tile, (near, fft)) for tile in range(3)]
    def follow(when):
        for tile in range(3):
            if SECOND[tile] == when:
                second[tile].start()

    for copy in first:
        copy.start()
    follow("a")

    mine, mate, after = grids.at[0], grids.at[1], grids.at[2]
    chunks = [(0, pl.ds(0, PACKED)), (1, pl.ds(0, CUT)), (1, pl.ds(CUT, PACKED - CUT))]
    peers = [(orb, other), (near, other), (near, other)]
    halves = [
        send(spectra.at[pair, 1 - core, rows], arrived.at[pair, rows],
             half_send.at[place], half_recv.at[place], peers[place])
        for place, (pair, rows) in enumerate(chunks)
    ]
    fars = [
        send(summed.at[pair, rows], crossed.at[pair, rows],
             far_send.at[place], far_recv.at[place], (orb, far))
        for place, (pair, rows) in enumerate(chunks)
    ]

    asides = [
        send(summed.at[pair, rows], passing.at[pair, rows],
             aside_send.at[place], aside_recv.at[place], (aside, fft))
        for place, (pair, rows) in enumerate(chunks)
    ]
    onward = [
        send(passing.at[pair, rows], crossed.at[pair, rows],
             aside_send.at[place], far_recv.at[place], (aside, far))
        for place, (pair, rows) in enumerate(chunks)
    ]

    def give(place, slot, field, half, peer):
        pair, rows = chunks[place]
        return send(fields.at[pair, half, rows], fields.at[field, half, rows],
                    give_send.at[place, slot], give_recv.at[place, slot], peer)

    gives = [[give(0, 0, 0, core, (orb, other))]]
    for place in (1, 2):
        gives.append([give(place, 0, 1, core, (near, other)), give(place, 1, 2, core, (orb, other)),
                      give(place, 2, 2, 1 - core, (orb, other))])

    def cross(place):
        pair, rows = chunks[place]
        halves[place].wait_recv()
        summed[pair, rows] = spectra[pair, core, rows] + arrived[pair, rows]
        if place in ASIDE:
            pl.when(inner)(fars[place].start)
            pl.when(jnp.logical_not(inner))(asides[place].start)
        else:
            fars[place].start()

    def pass_on(place):
        if place in ASIDE:
            @pl.when(inner)
            def _():
                asides[place].wait_recv()
                onward[place].start()

    def hand_out(place):
        pair, rows = chunks[place]
        fars[place].wait_recv()
        fields[pair, core, rows] = summed[pair, rows] + crossed[pair, rows]
        for copy in gives[place][:2]:
            copy.start()

    for load in loads:
        load.wait()
    fill_coulomb(depth, pick, coulomb, limits)
    for tile in range(3):
        spread(own, mine, tile)
        forward_y(mine, mine, t1, u, tile)
        forward_x(u, t2, f, tile)
    forward_z(f, t3, coulomb, spectra.at[0])
    halves[0].start()
    if OWN_CROSS == "early":
        cross(0)

    for tile in range(3):
        first[tile].wait_recv()
        if tile == 2:
            if OWN_CROSS == "arrived":
                cross(0)
            follow("b")
        spread(raw.at[0], mate, tile)
        forward_y(mine, mate, t1, u, tile)
        forward_x(u, t2, f, tile)
    forward_z(f, t3, coulomb, spectra.at[1])
    if PASS_OWN == "sent":
        pass_on(0)
    halves[1].start()
    halves[2].start()
    follow("c")
    if OWN_CROSS == "sent":
        cross(0)
    cross(1)
    cross(2)
    if OWN_CROSS == "last":
        cross(0)
    follow("d")
    if PASS_OWN == "crossed":
        pass_on(0)
    pass_on(1)
    if PASS_LAST == "crossed":
        pass_on(2)

    hand_out(0)
    gives[0][0].wait_recv()
    backward_z(fields.at[0], t3b, f)
    backward_x(f, t2b, u)
    for tile in range(3):
        backward_y((u,), t1b, (mine,), total, True, tile)

    if PASS_LAST == "own":
        pass_on(2)
    hand_out(1)
    follow("e")
    hand_out(2)
    follow("f")
    def arrive(when):
        if SPREAD == when:
            for tile in range(3):
                second[tile].wait_recv()
                spread(raw.at[1], after, tile)

    arrive("first")
    for place in (1, 2):
        gives[place][0].wait_recv()
        gives[place][2].start()
    arrive("second")
    backward_z(fields.at[1], t3b, f)
    backward_x(f, t2b, u)
    arrive("third")
    for place in (1, 2):
        gives[place][1].wait_recv()
        gives[place][2].wait_recv()
    backward_z(fields.at[2], t3b, f)
    backward_x(f, t2b, u2)
    arrive("last")
    for tile in range(3):
        backward_y((u, u2), t1b, (mate, after), total, False, tile)
        gather(total, out, tile)
    for copy in first + second + halves + sum(gives, []):
        copy.wait_send()
    for place in range(3):
        if place in ASIDE:
            @pl.when(inner)
            def _():
                fars[place].wait_send()
                onward[place].wait_send()

            pl.when(jnp.logical_not(inner))(asides[place].wait_send)
        else:
            fars[place].wait_send()


def shards(orbitals, sphere_depth):
    t1, t2, t3, t3b, t2b, t1b, pick = make_tables()
    vmem = pl.BlockSpec(memory_space=pltpu.VMEM)
    cells = PLANES * NG * NG // 128
    dma = pltpu.SemaphoreType.DMA
    tiled = orbitals.reshape(PLANES // 8, 8, NG * NG // 128, 128).transpose(0, 2, 1, 3).reshape(cells, 128)
    result = pl.pallas_call(
        kernel,
        out_shape=pltpu.VMEM((cells, 128), F32),
        in_specs=[pl.BlockSpec(memory_space=pltpu.HBM)] * 9,
        out_specs=vmem,
        scratch_shapes=[
            pltpu.VMEM((cells, 128), F32),
            pltpu.VMEM(sphere_depth.shape, jnp.int32),
            pltpu.VMEM(t1.shape, BF),
            pltpu.VMEM(t2.shape, BF),
            pltpu.VMEM(t3.shape[1:], BF),
            pltpu.VMEM(t3b.shape[1:], BF),
            pltpu.VMEM(t2b.shape, BF),
            pltpu.VMEM(t1b.shape, BF),
            pltpu.VMEM(pick.shape, F32),
            dma((9,)),
            pltpu.VMEM((2, cells, 128), F32),
            pltpu.VMEM((3, PLANES * PITCH, 128), F32),
            pltpu.VMEM((PLANES * PITCH, 128), F32),
            pltpu.VMEM((2, HALF * PLANES, 128), F32),
            pltpu.VMEM((2, HALF * PLANES, 128), F32),
            pltpu.VMEM((HALF * PLANES, 128), F32),
            pltpu.VMEM((HALF * ROWS, 128), F32),
            pltpu.VMEM((NG, 128), F32),
            pltpu.VMEM((2, 2, PACKED, 128), F32),
            pltpu.VMEM((2, PACKED, 128), F32),
            pltpu.VMEM((2, PACKED, 128), F32),
            pltpu.VMEM((2, PACKED, 128), F32),
            pltpu.VMEM((2, PACKED, 128), F32),
            pltpu.VMEM((3, 2, PACKED, 128), F32),
            dma((2, 3)), dma((2, 3)), dma((3,)), dma((3,)), dma((3,)), dma((3,)), dma((3,)), dma((3,)), dma((3, 3)), dma((3, 3)),
        ],
        compiler_params=pltpu.CompilerParams(
            collective_id=0, has_side_effects=True, vmem_limit_bytes=60 << 20
        ),
        cost_estimate=pl.CostEstimate(flops=10**9, bytes_accessed=4 * 10**6, transcendentals=0),
    )(
        tiled, sphere_depth,
        jnp.asarray(t1), jnp.asarray(t2), jnp.asarray(t3), jnp.asarray(t3b),
        jnp.asarray(t2b), jnp.asarray(t1b), jnp.asarray(pick),
    )
    result = result.reshape(PLANES // 8, NG * NG // 128, 8, 128)
    return result.transpose(0, 2, 1, 3).reshape(orbitals.shape)


def solution(mesh):
    placed = (P("orb", "fft", None), P())
    return jax.shard_map(
        shards, mesh=mesh, in_specs=placed, out_specs=P("orb", "fft", None), check_vma=False
    )
```

```python
import functools
import math

import jax
import jax.numpy as jnp
import ml_dtypes
import numpy as np
from jax import lax
from jax.experimental import pallas as pl
from jax.experimental.pallas import tpu as pltpu
from jax.sharding import PartitionSpec as P

NG = 96
PLANES = 24
HALF = 24
PITCH = 104
ROWS = 48
CROP = 23
UNROLL = dict(spread=24, gather=24, forward_y=4, backward_x=4, backward_y=4)
COULOMB = 0.1
BF = jnp.bfloat16
F32 = jnp.float32
MESH = pl.DeviceIdType.MESH


def signed_order(count):
    place = np.arange(count)
    size = (place + 1) // 2
    return np.where(place % 2 == 1, size, -size)


def angle(a, b):
    return 2.0 * math.pi / NG * (np.outer(a, b) % NG)


def half_of(ky):
    return int(ky % 4 in (1, 2))


def pack_blocks():
    place, most = {}, 0
    for half in range(2):
        filled = 0
        for ky in range(HALF):
            for m in range(ROWS // 8):
                left = CROP**2 - ky**2 - (4 * m) ** 2
                if half_of(ky) != half or left < 0:
                    continue
                width = 2 * math.isqrt(left) + 1
                tile, start = divmod(filled, 64)
                end = start + width
                place[ky, m] = [(half, tile, start, start, min(end, 64))]
                if end > 64:
                    place[ky, m].append((half, tile + 1, start + 64, 0, end - 64))
                filled += width
        most = max(most, -(-filled // 64))
    return place, most


PLACE, TILES = pack_blocks()
PACKED = TILES * 8
OWN_CROSS = "early"
STRAIGHT = False
DIRECT = True
PARTS = 3
SECOND = "ccc"
CHUNKS = 5
SPREAD = "first"
ASIDE = (0, 1, 2, 3, 4)
PASS_OWN = "crossed"


def split_table(table):
    high = table.astype(ml_dtypes.bfloat16)
    low = (table - high.astype(np.float64)).astype(ml_dtypes.bfloat16)
    return high, low


def make_tables():
    grid = np.arange(NG)
    ky = np.arange(HALF)
    a = angle(ky, grid)
    hi, lo = split_table(np.concatenate([np.cos(a), -np.sin(a)], 0))
    t1 = np.block([[hi, hi], [lo, lo]])

    kx = signed_order(47)
    a = np.zeros((128, 64))
    c, s = np.zeros((128, 64)), np.zeros((128, 64))
    c[:NG, :47] = np.cos(angle(grid, kx))
    s[:NG, :47] = np.sin(angle(grid, kx))
    hi, lo = split_table(np.block([[c, -s], [s, c]]))
    t2 = np.concatenate([hi, lo], 1)
    hi, lo = split_table(np.block([[c.T, s.T], [-s.T, c.T]]))
    t2b = np.concatenate([hi, hi, lo], 0)

    weight = np.where(ky == 0, 1.0, 2.0) / float(NG**3)
    a = angle(grid, ky)
    hi, lo = split_table(np.concatenate([np.cos(a) * weight, -np.sin(a) * weight], 1))
    t1b = np.concatenate([hi, hi, lo], 1)

    kz = signed_order(ROWS)
    t3, t3b = [], []
    for slab in range(NG // PLANES):
        z = slab * PLANES + np.arange(PLANES)
        a = angle(kz, z)
        hi, lo = split_table(np.concatenate([np.cos(a), np.sin(a)], 0))
        t3.append(np.concatenate([hi, hi, lo, lo], 1))
        a = angle(z, kz)
        hi, lo = split_table(np.concatenate([np.cos(a), np.sin(a)], 0))
        t3b.append(np.concatenate([hi, hi, lo], 1))
    pick = np.zeros((HALF, 128), np.float32)
    for lane in range(128):
        if lane % 64 < 47:
            pick[abs(kx[lane % 64]), lane] = 1.0
    return t1, t2, np.stack(t3), np.stack(t3b), t2b, t1b, pick


def lanes(rows):
    return lax.broadcasted_iota(jnp.int32, (rows, 128), 1)


def split(value):
    high = value.astype(BF)
    return high, (value - high.astype(F32)).astype(BF)


def dot(a, b):
    return jnp.dot(a, b, preferred_element_type=F32)


def spread(raw, grid, tile):
    row = tile * 8
    lane = lanes(8)

    @pl.loop(0, NG // 4, unroll=UNROLL["spread"])
    def _(group):
        start = tile * 576 + pl.multiple_of(group * 24, 24)
        t0, t1, t2 = [raw[pl.ds(start + 8 * k, 8), :] for k in range(3)]
        pieces = (
            t0,
            pltpu.roll(jnp.where(lane >= 96, t0, t1), 32, 1),
            pltpu.roll(jnp.where(lane >= 64, t1, t2), 64, 1),
            pltpu.roll(t2, 96, 1),
        )
        for j, piece in enumerate(pieces):
            grid[pl.ds(row * PITCH + group * 4 + j, 8, stride=PITCH), :] = piece


def gather(grid, out, tile):
    lane = lanes(8)

    @pl.loop(0, NG // 4, unroll=UNROLL["gather"])
    def _(group):
        a = [grid[pl.ds(tile * 8 * PITCH + group * 4 + j, 8, stride=PITCH), :] for j in range(4)]
        r1, r2, r3 = pltpu.roll(a[1], 96, 1), pltpu.roll(a[2], 64, 1), pltpu.roll(a[3], 32, 1)
        start = tile * 576 + pl.multiple_of(group * 24, 24)
        out[pl.ds(start, 8), :] = jnp.where(lane < 96, a[0], r1)
        out[pl.ds(start + 8, 8), :] = jnp.where(lane < 64, r1, r2)
        out[pl.ds(start + 16, 8), :] = jnp.where(lane < 32, r2, r3)


def forward_y(left, right, t1, u, tile):
    @pl.loop(tile * 4, tile * 4 + 4, unroll=UNROLL["forward_y"])
    def _(pair):
        planes = [pl.ds(pl.multiple_of((pair * 2 + t) * PITCH, PITCH), NG) for t in range(2)]
        hi, lo = split(jnp.concatenate([left[rows, :] * right[rows, :] for rows in planes], 1))
        o = dot(t1[...], jnp.concatenate([hi, lo], 0))
        o = o[:48] + o[48:]
        for t in range(2):
            where = pl.ds(pair * 2 + t, HALF, stride=PLANES)
            u.at[0][where, :] = o[:24, 128 * t : 128 * t + 128]
            u.at[1][where, :] = o[24:, 128 * t : 128 * t + 128]


def forward_x(u, t2, f, tile):
    places = [pl.ds(ky * PLANES + tile * 8, 8) for ky in range(HALF)]
    parts = [jnp.concatenate([u[c, where, :] for where in places], 0) for c in range(2)]
    hi, lo = split(jnp.concatenate(parts, 1))
    o = dot(hi, t2[...])
    o = o[:, :128] + o[:, 128:] + dot(lo, t2[:, :128])
    for ky, where in enumerate(places):
        f[where, :] = o[8 * ky : 8 * ky + 8]


def forward_z(f, t3, coulomb, spectrum):
    sign = jnp.where(lanes(ROWS) < 64, 1.0, -1.0)
    lane = lanes(8) % 64
    written = set()
    for pair in range(HALF // 2):
        v = f[pl.ds(pair * 48, 48), :]
        v = jnp.concatenate([v[:24], v[24:]], 1)
        hi = v.astype(BF).astype(F32)
        lo = v - hi
        o = dot(t3[...], jnp.concatenate([hi, lo, hi, lo], 0).astype(BF))
        for t in range(2):
            ky = pair * 2 + t
            part = o[:, 128 * t : 128 * t + 128]
            part = part[:48] + sign * pltpu.roll(part[48:], 64, 1)
            part = part * coulomb[pl.ds(ky * ROWS, ROWS), :]
            for m in range(ROWS // 8):
                if (ky, m) not in PLACE:
                    continue
                for half, tile, shift, low, high in PLACE[ky, m]:
                    block = part[8 * m : 8 * m + 8]
                    if shift:
                        block = pltpu.roll(block, shift, 1)
                    if len(PLACE[ky, m]) > 1:
                        block = jnp.where((lane >= low) & (lane < high), block, 0.0)
                    rows = pl.ds(tile * 8, 8)
                    if (half, tile) in written:
                        block = block + spectrum[half, rows, :]
                    spectrum[half, rows, :] = block
                    written.add((half, tile))
    for half in range(2):
        for tile in range(TILES):
            if (half, tile) not in written:
                spectrum[half, pl.ds(tile * 8, 8), :] = jnp.zeros((8, 128), F32)


def backward_z(spectrum, t3b, f):
    sign = jnp.where(lanes(PLANES) < 64, -1.0, 1.0)
    lane = lanes(8) % 64
    none = jnp.zeros((8, 128), F32)

    def unpacked(ky):
        blocks = []
        for m in range(ROWS // 8):
            if (ky, m) not in PLACE:
                blocks.append(none)
                continue
            total = None
            for half, tile, shift, low, high in PLACE[ky, m]:
                block = jnp.where((lane >= low) & (lane < high), spectrum[half, pl.ds(tile * 8, 8), :], 0.0)
                if shift:
                    block = pltpu.roll(block, 128 - shift, 1)
                total = block if total is None else total + block
            blocks.append(total)
        return jnp.concatenate(blocks, 0)

    for pair in range(HALF // 2):
        hi, lo = split(jnp.concatenate([unpacked(pair * 2), unpacked(pair * 2 + 1)], 1))
        o = dot(t3b[...], jnp.concatenate([hi, lo, hi], 0))
        for t in range(2):
            part = o[:, 128 * t : 128 * t + 128]
            f[pl.ds(pair * 48 + 24 * t, 24), :] = part[:24] + sign * pltpu.roll(part[24:], 64, 1)


def backward_x(f, t2b, u):
    @pl.loop(0, 4, unroll=UNROLL["backward_x"])
    def _(block):
        rows = pl.ds(pl.multiple_of(block * 144, 144), 144)
        hi, lo = split(f[rows, :])
        o = dot(jnp.concatenate([hi, lo], 1), t2b[:256, :]) + dot(hi, t2b[256:, :])
        u[0, rows, :] = o[:, :128]
        u[1, rows, :] = o[:, 128:]


def backward_y(fields, t1b, orbitals, total, fresh, tile):
    @pl.loop(tile * 4, tile * 4 + 4, unroll=UNROLL["backward_y"])
    def _(pair):
        terms = [None, None]
        for u, orbital in zip(fields, orbitals):
            parts = []
            for t in range(2):
                where = pl.ds(pair * 2 + t, HALF, stride=PLANES)
                parts.append(jnp.concatenate([u.at[0][where, :], u.at[1][where, :]], 0))
            hi, lo = split(jnp.concatenate(parts, 1))
            v = dot(t1b[...], jnp.concatenate([hi, lo, hi], 0))
            for t in range(2):
                rows = pl.ds(pl.multiple_of((pair * 2 + t) * PITCH, PITCH), NG)
                term = orbital[rows, :] * v[:, 128 * t : 128 * t + 128]
                terms[t] = term if terms[t] is None else terms[t] + term
        for t in range(2):
            rows = pl.ds(pl.multiple_of((pair * 2 + t) * PITCH, PITCH), NG)
            total[rows, :] = terms[t] if fresh else total[rows, :] + terms[t]


def fill_coulomb(depth, pick, coulomb, limits):
    kept = depth[...].astype(F32)[:HALF] + 1.0
    limits[...] = lax.dot_general(
        kept, pick[...], (((0,), (0,)), ((), ())), preferred_element_type=F32
    ) - 1.0
    lane = lax.broadcasted_iota(jnp.int32, (ROWS, 128), 1) % 64
    row = lax.broadcasted_iota(jnp.int32, (ROWS, 128), 0)
    kx, kz = (lane + 1) // 2, (row + 1) // 2
    square = (kx * kx + kz * kz).astype(F32)
    size = kz.astype(F32)

    @pl.loop(0, HALF, unroll=4)
    def _(ky):
        whole = square + (ky * ky).astype(F32)
        inside = (size <= limits[pl.ds(ky, 1), :]) & (whole > 0.5)
        coulomb[pl.ds(pl.multiple_of(ky * ROWS, ROWS), ROWS), :] = jnp.where(
            inside, COULOMB * NG**1.5 / jnp.maximum(whole, 1.0), 0.0
        )


def kernel(
    own_hbm, depth_hbm, t1_hbm, t2_hbm, t3_hbm, t3b_hbm, t2b_hbm, t1b_hbm, pick_hbm, out,
    own, depth, t1, t2, t3, t3b, t2b, t1b, pick, load_sem, raw, grids, total, u, u2, f, coulomb, limits,
    spectra, arrived, summed, passing, crossed, fields,
    phi_send, phi_recv, half_send, half_recv, far_send, far_recv, aside_send, aside_recv, give_send, give_recv,
):
    orb, fft = lax.axis_index("orb"), lax.axis_index("fft")
    blocks = lax.axis_size("orb")
    core = fft % 2
    other = fft + 1 - 2 * core
    far = (fft + 2) % 4
    near = (orb + blocks - 1 + 2 * core) % blocks
    back = (orb + 1 - 2 * core) % blocks
    aside = orb + 1 - 2 * (orb % 2)
    inner = (orb % 4 + 1) % 4 >= 2

    def distant(place_on_ring):
        return place_on_ring % 16 == 15 * core

    def straight(place):
        return inner | distant(orb) if place and STRAIGHT else inner

    def relays(place):
        return inner & jnp.logical_not(distant(aside)) if place and STRAIGHT else inner

    loads = [
        pltpu.make_async_copy(src, dst, load_sem.at[place])
        for place, (src, dst) in enumerate((
            (own_hbm, own), (depth_hbm, depth), (pick_hbm, pick), (t1_hbm, t1), (t2_hbm, t2),
            (t3_hbm.at[fft], t3), (t3b_hbm.at[fft], t3b), (t2b_hbm, t2b), (t1b_hbm, t1b),
        ))
    ]
    for load in loads:
        load.start()

    barrier = pltpu.get_barrier_semaphore()
    for peer in ((near, fft), (back, fft), (orb, other), (near, other), (orb, far), (aside, far)):
        pl.semaphore_signal(barrier, inc=1, device_id=peer, device_id_type=MESH)
    pl.semaphore_wait(barrier, 6)

    def send(src, dst, send_sem, recv_sem, peer):
        return pltpu.make_async_remote_copy(
            src_ref=src, dst_ref=dst, send_sem=send_sem, recv_sem=recv_sem,
            device_id=peer, device_id_type=MESH,
        )

    def orbital_copy(phase, part, size, peer):
        rows = pl.ds(part * size, size)
        return send(own_hbm.at[rows], raw.at[phase, rows], phi_send.at[phase, part],
                    phi_recv.at[phase, part], peer)

    first = [orbital_copy(0, part, 576, (back, fft)) for part in range(3)]
    second = [orbital_copy(1, part, 1728 // PARTS, (near, fft)) for part in range(PARTS)]
    def follow(when):
        for part in range(PARTS):
            if SECOND[part] == when:
                second[part].start()

    for copy in first:
        copy.start()
    follow("a")

    mine, mate, after = grids.at[0], grids.at[1], grids.at[2]
    chunks = [(0, pl.ds(0, PACKED))] + [(1, pl.ds(PACKED // CHUNKS * k, PACKED // CHUNKS)) for k in range(CHUNKS)]
    peers = [(orb, other)] + [(near, other)] * CHUNKS
    halves = [
        send(spectra.at[pair, 1 - core, rows], arrived.at[pair, rows],
             half_send.at[place], half_recv.at[place], peers[place])
        for place, (pair, rows) in enumerate(chunks)
    ]
    fars = [
        send(summed.at[pair, rows], crossed.at[pair, rows],
             far_send.at[place], far_recv.at[place], (orb, far))
        for place, (pair, rows) in enumerate(chunks)
    ]

    asides = [
        send(summed.at[pair, rows], passing.at[pair, rows],
             aside_send.at[place], aside_recv.at[place], (aside, fft))
        for place, (pair, rows) in enumerate(chunks)
    ]
    onward = [
        send(passing.at[pair, rows], crossed.at[pair, rows],
             aside_send.at[place], far_recv.at[place], (aside, far))
        for place, (pair, rows) in enumerate(chunks)
    ]

    def give(place, slot, field, half, peer):
        pair, rows = chunks[place]
        return send(fields.at[pair, half, rows], fields.at[field, half, rows],
                    give_send.at[place, slot], give_recv.at[place, slot], peer)

    gives = [[give(0, 0, 0, core, (orb, other))]]
    for place in range(1, CHUNKS + 1):
        gives.append([give(place, 0, 1, core, (near, other)), give(place, 1, 2, core, (orb, other)),
                      give(place, 2, 2, core, (near, fft)) if DIRECT else give(place, 2, 2, 1 - core, (orb, other))])

    def cross(place):
        pair, rows = chunks[place]
        halves[place].wait_recv()
        summed[pair, rows] = spectra[pair, core, rows] + arrived[pair, rows]
        if place in ASIDE:
            pl.when(straight(place))(fars[place].start)
            pl.when(jnp.logical_not(straight(place)))(asides[place].start)
        else:
            fars[place].start()

    def pass_on(place):
        if place in ASIDE:
            @pl.when(relays(place))
            def _():
                asides[place].wait_recv()
                onward[place].start()

    def hand_out(place):
        pair, rows = chunks[place]
        fars[place].wait_recv()
        fields[pair, core, rows] = summed[pair, rows] + crossed[pair, rows]
        for copy in gives[place] if DIRECT else gives[place][:2]:
            copy.start()

    for load in loads:
        load.wait()
    fill_coulomb(depth, pick, coulomb, limits)
    for tile in range(3):
        spread(own, mine, tile)
        forward_y(mine, mine, t1, u, tile)
        forward_x(u, t2, f, tile)
    forward_z(f, t3, coulomb, spectra.at[0])
    halves[0].start()
    if OWN_CROSS == "early":
        cross(0)

    for tile in range(3):
        first[tile].wait_recv()
        if tile == 2:
            if OWN_CROSS == "arrived":
                cross(0)
            follow("b")
        spread(raw.at[0], mate, tile)
        forward_y(mine, mate, t1, u, tile)
        forward_x(u, t2, f, tile)
    forward_z(f, t3, coulomb, spectra.at[1])
    if PASS_OWN == "sent":
        pass_on(0)
    for place in range(1, CHUNKS + 1):
        halves[place].start()
    follow("c")
    if OWN_CROSS == "sent":
        cross(0)
    for place in range(1, CHUNKS + 1):
        cross(place)
    if OWN_CROSS == "last":
        cross(0)
    follow("d")
    if PASS_OWN == "crossed":
        pass_on(0)
    for place in range(1, CHUNKS + 1):
        pass_on(place)

    hand_out(0)
    gives[0][0].wait_recv()
    backward_z(fields.at[0], t3b, f)
    backward_x(f, t2b, u)
    for tile in range(3):
        backward_y((u,), t1b, (mine,), total, True, tile)

    for place in range(1, CHUNKS + 1):
        hand_out(place)
        if place == 1:
            follow("e")

    def arrive(when):
        if SPREAD == when:
            for tile in range(3):
                for part in range(PARTS):
                    if part * 3 // PARTS == tile:
                        second[part].wait_recv()
                spread(raw.at[1], after, tile)

    arrive("first")
    for place in range(1, CHUNKS + 1):
        gives[place][0].wait_recv()
        if not DIRECT:
            gives[place][2].start()
    arrive("second")
    backward_z(fields.at[1], t3b, f)
    backward_x(f, t2b, u)
    arrive("third")
    for place in range(1, CHUNKS + 1):
        gives[place][1].wait_recv()
        gives[place][2].wait_recv()
    backward_z(fields.at[2], t3b, f)
    backward_x(f, t2b, u2)
    arrive("last")
    for tile in range(3):
        backward_y((u, u2), t1b, (mate, after), total, False, tile)
        gather(total, out, tile)
    for copy in first + second + halves + sum(gives, []):
        copy.wait_send()
    for place in range(CHUNKS + 1):
        if place in ASIDE:
            pl.when(straight(place))(fars[place].wait_send)
            pl.when(relays(place))(onward[place].wait_send)
            pl.when(jnp.logical_not(straight(place)))(asides[place].wait_send)
        else:
            fars[place].wait_send()


def shards(orbitals, sphere_depth):
    t1, t2, t3, t3b, t2b, t1b, pick = make_tables()
    vmem = pl.BlockSpec(memory_space=pltpu.VMEM)
    cells = PLANES * NG * NG // 128
    dma = pltpu.SemaphoreType.DMA
    tiled = orbitals.reshape(PLANES // 8, 8, NG * NG // 128, 128).transpose(0, 2, 1, 3).reshape(cells, 128)
    result = pl.pallas_call(
        kernel,
        out_shape=pltpu.VMEM((cells, 128), F32),
        in_specs=[pl.BlockSpec(memory_space=pltpu.HBM)] * 9,
        out_specs=vmem,
        scratch_shapes=[
            pltpu.VMEM((cells, 128), F32),
            pltpu.VMEM(sphere_depth.shape, jnp.int32),
            pltpu.VMEM(t1.shape, BF),
            pltpu.VMEM(t2.shape, BF),
            pltpu.VMEM(t3.shape[1:], BF),
            pltpu.VMEM(t3b.shape[1:], BF),
            pltpu.VMEM(t2b.shape, BF),
            pltpu.VMEM(t1b.shape, BF),
            pltpu.VMEM(pick.shape, F32),
            dma((9,)),
            pltpu.VMEM((2, cells, 128), F32),
            pltpu.VMEM((3, PLANES * PITCH, 128), F32),
            pltpu.VMEM((PLANES * PITCH, 128), F32),
            pltpu.VMEM((2, HALF * PLANES, 128), F32),
            pltpu.VMEM((2, HALF * PLANES, 128), F32),
            pltpu.VMEM((HALF * PLANES, 128), F32),
            pltpu.VMEM((HALF * ROWS, 128), F32),
            pltpu.VMEM((NG, 128), F32),
            pltpu.VMEM((2, 2, PACKED, 128), F32),
            pltpu.VMEM((2, PACKED, 128), F32),
            pltpu.VMEM((2, PACKED, 128), F32),
            pltpu.VMEM((2, PACKED, 128), F32),
            pltpu.VMEM((2, PACKED, 128), F32),
            pltpu.VMEM((3, 2, PACKED, 128), F32),
            *[dma((2, max(PARTS, 3)))] * 2, *[dma((CHUNKS + 1,))] * 6, *[dma((CHUNKS + 1, 3))] * 2,
        ],
        compiler_params=pltpu.CompilerParams(
            collective_id=0, has_side_effects=True, vmem_limit_bytes=60 << 20
        ),
        cost_estimate=pl.CostEstimate(flops=10**9, bytes_accessed=4 * 10**6, transcendentals=0),
    )(
        tiled, sphere_depth,
        jnp.asarray(t1), jnp.asarray(t2), jnp.asarray(t3), jnp.asarray(t3b),
        jnp.asarray(t2b), jnp.asarray(t1b), jnp.asarray(pick),
    )
    result = result.reshape(PLANES // 8, NG * NG // 128, 8, 128)
    return result.transpose(0, 2, 1, 3).reshape(orbitals.shape)


def solution(mesh):
    placed = (P("orb", "fft", None), P())
    return jax.shard_map(
        shards, mesh=mesh, in_specs=placed, out_specs=P("orb", "fft", None), check_vma=False
    )
```

```python
import functools
import math

import jax
import jax.numpy as jnp
import ml_dtypes
import numpy as np
from jax import lax
from jax.experimental import pallas as pl
from jax.experimental.pallas import tpu as pltpu
from jax.sharding import PartitionSpec as P

NG = 96
PLANES = 24
HALF = 24
PITCH = 104
ROWS = 48
CROP = 23
UNROLL = dict(spread=24, gather=24, forward_y=4, backward_x=4, backward_y=4)
COULOMB = 0.1
BF = jnp.bfloat16
F32 = jnp.float32
MESH = pl.DeviceIdType.MESH


def signed_order(count):
    place = np.arange(count)
    size = (place + 1) // 2
    return np.where(place % 2 == 1, size, -size)


def angle(a, b):
    return 2.0 * math.pi / NG * (np.outer(a, b) % NG)


def half_of(ky):
    return int(ky % 4 in (1, 2))


def pack_blocks():
    place, most = {}, 0
    for half in range(2):
        filled = 0
        for ky in range(HALF):
            for m in range(ROWS // 8):
                left = CROP**2 - ky**2 - (4 * m) ** 2
                if half_of(ky) != half or left < 0:
                    continue
                width = 2 * math.isqrt(left) + 1
                tile, start = divmod(filled, 64)
                end = start + width
                place[ky, m] = [(half, tile, start, start, min(end, 64))]
                if end > 64:
                    place[ky, m].append((half, tile + 1, start + 64, 0, end - 64))
                filled += width
        most = max(most, -(-filled // 64))
    return place, most


PLACE, TILES = pack_blocks()
PACKED = TILES * 8
OWN_CROSS = "early"
STRAIGHT = False
DIRECT = True
PARTS = 3
SECOND = "ccc"
CHUNKS = 5
SPREAD = "first"
ASIDE = (0, 1, 2, 3, 4)
PASS_OWN = "crossed"


def split_table(table):
    high = table.astype(ml_dtypes.bfloat16)
    low = (table - high.astype(np.float64)).astype(ml_dtypes.bfloat16)
    return high, low


def make_tables():
    grid = np.arange(NG)
    ky = np.arange(HALF)
    a = angle(ky, grid)
    hi, lo = split_table(np.concatenate([np.cos(a), -np.sin(a)], 0))
    t1 = np.block([[hi, hi], [lo, lo]])

    kx = signed_order(47)
    a = np.zeros((128, 64))
    c, s = np.zeros((128, 64)), np.zeros((128, 64))
    c[:NG, :47] = np.cos(angle(grid, kx))
    s[:NG, :47] = np.sin(angle(grid, kx))
    hi, lo = split_table(np.block([[c, -s], [s, c]]))
    t2 = np.concatenate([hi, lo], 1)
    hi, lo = split_table(np.block([[c.T, s.T], [-s.T, c.T]]))
    t2b = np.concatenate([hi, hi, lo], 0)

    weight = np.where(ky == 0, 1.0, 2.0) / float(NG**3)
    a = angle(grid, ky)
    hi, lo = split_table(np.concatenate([np.cos(a) * weight, -np.sin(a) * weight], 1))
    t1b = np.concatenate([hi, hi, lo], 1)

    kz = signed_order(ROWS)
    t3, t3b = [], []
    for slab in range(NG // PLANES):
        z = slab * PLANES + np.arange(PLANES)
        a = angle(kz, z)
        hi, lo = split_table(np.concatenate([np.cos(a), np.sin(a)], 0))
        t3.append(np.concatenate([hi, hi, lo, lo], 1))
        a = angle(z, kz)
        hi, lo = split_table(np.concatenate([np.cos(a), np.sin(a)], 0))
        t3b.append(np.concatenate([hi, hi, lo], 1))
    pick = np.zeros((HALF, 128), np.float32)
    for lane in range(128):
        if lane % 64 < 47:
            pick[abs(kx[lane % 64]), lane] = 1.0
    return t1, t2, np.stack(t3), np.stack(t3b), t2b, t1b, pick


def lanes(rows):
    return lax.broadcasted_iota(jnp.int32, (rows, 128), 1)


def split(value):
    high = value.astype(BF)
    return high, (value - high.astype(F32)).astype(BF)


def dot(a, b):
    return jnp.dot(a, b, preferred_element_type=F32)


def spread(raw, grid, tile):
    row = tile * 8
    lane = lanes(8)

    @pl.loop(0, NG // 4, unroll=UNROLL["spread"])
    def _(group):
        start = tile * 576 + pl.multiple_of(group * 24, 24)
        t0, t1, t2 = [raw[pl.ds(start + 8 * k, 8), :] for k in range(3)]
        pieces = (
            t0,
            pltpu.roll(jnp.where(lane >= 96, t0, t1), 32, 1),
            pltpu.roll(jnp.where(lane >= 64, t1, t2), 64, 1),
            pltpu.roll(t2, 96, 1),
        )
        for j, piece in enumerate(pieces):
            grid[pl.ds(row * PITCH + group * 4 + j, 8, stride=PITCH), :] = piece


def gather(grid, out, tile):
    lane = lanes(8)

    @pl.loop(0, NG // 4, unroll=UNROLL["gather"])
    def _(group):
        a = [grid[pl.ds(tile * 8 * PITCH + group * 4 + j, 8, stride=PITCH), :] for j in range(4)]
        r1, r2, r3 = pltpu.roll(a[1], 96, 1), pltpu.roll(a[2], 64, 1), pltpu.roll(a[3], 32, 1)
        start = tile * 576 + pl.multiple_of(group * 24, 24)
        out[pl.ds(start, 8), :] = jnp.where(lane < 96, a[0], r1)
        out[pl.ds(start + 8, 8), :] = jnp.where(lane < 64, r1, r2)
        out[pl.ds(start + 16, 8), :] = jnp.where(lane < 32, r2, r3)


def forward_y(left, right, t1, u, tile):
    @pl.loop(tile * 4, tile * 4 + 4, unroll=UNROLL["forward_y"])
    def _(pair):
        planes = [pl.ds(pl.multiple_of((pair * 2 + t) * PITCH, PITCH), NG) for t in range(2)]
        hi, lo = split(jnp.concatenate([left[rows, :] * right[rows, :] for rows in planes], 1))
        o = dot(t1[...], jnp.concatenate([hi, lo], 0))
        o = o[:48] + o[48:]
        for t in range(2):
            where = pl.ds(pair * 2 + t, HALF, stride=PLANES)
            u.at[0][where, :] = o[:24, 128 * t : 128 * t + 128]
            u.at[1][where, :] = o[24:, 128 * t : 128 * t + 128]


def forward_x(u, t2, f, tile):
    places = [pl.ds(ky * PLANES + tile * 8, 8) for ky in range(HALF)]
    parts = [jnp.concatenate([u[c, where, :] for where in places], 0) for c in range(2)]
    hi, lo = split(jnp.concatenate(parts, 1))
    o = dot(hi, t2[...])
    o = o[:, :128] + o[:, 128:] + dot(lo, t2[:, :128])
    for ky, where in enumerate(places):
        f[where, :] = o[8 * ky : 8 * ky + 8]


def forward_z(f, t3, coulomb, spectrum):
    sign = jnp.where(lanes(ROWS) < 64, 1.0, -1.0)
    lane = lanes(8) % 64
    written = set()
    for pair in range(HALF // 2):
        v = f[pl.ds(pair * 48, 48), :]
        v = jnp.concatenate([v[:24], v[24:]], 1)
        hi = v.astype(BF).astype(F32)
        lo = v - hi
        o = dot(t3[...], jnp.concatenate([hi, lo, hi, lo], 0).astype(BF))
        for t in range(2):
            ky = pair * 2 + t
            part = o[:, 128 * t : 128 * t + 128]
            part = part[:48] + sign * pltpu.roll(part[48:], 64, 1)
            part = part * coulomb[pl.ds(ky * ROWS, ROWS), :]
            for m in range(ROWS // 8):
                if (ky, m) not in PLACE:
                    continue
                for half, tile, shift, low, high in PLACE[ky, m]:
                    block = part[8 * m : 8 * m + 8]
                    if shift:
                        block = pltpu.roll(block, shift, 1)
                    if len(PLACE[ky, m]) > 1:
                        block = jnp.where((lane >= low) & (lane < high), block, 0.0)
                    rows = pl.ds(tile * 8, 8)
                    if (half, tile) in written:
                        block = block + spectrum[half, rows, :]
                    spectrum[half, rows, :] = block
                    written.add((half, tile))
    for half in range(2):
        for tile in range(TILES):
            if (half, tile) not in written:
                spectrum[half, pl.ds(tile * 8, 8), :] = jnp.zeros((8, 128), F32)


def backward_z(spectrum, t3b, f):
    sign = jnp.where(lanes(PLANES) < 64, -1.0, 1.0)
    lane = lanes(8) % 64
    none = jnp.zeros((8, 128), F32)

    def unpacked(ky):
        blocks = []
        for m in range(ROWS // 8):
            if (ky, m) not in PLACE:
                blocks.append(none)
                continue
            total = None
            for half, tile, shift, low, high in PLACE[ky, m]:
                block = jnp.where((lane >= low) & (lane < high), spectrum[half, pl.ds(tile * 8, 8), :], 0.0)
                if shift:
                    block = pltpu.roll(block, 128 - shift, 1)
                total = block if total is None else total + block
            blocks.append(total)
        return jnp.concatenate(blocks, 0)

    for pair in range(HALF // 2):
        hi, lo = split(jnp.concatenate([unpacked(pair * 2), unpacked(pair * 2 + 1)], 1))
        o = dot(t3b[...], jnp.concatenate([hi, lo, hi], 0))
        for t in range(2):
            part = o[:, 128 * t : 128 * t + 128]
            f[pl.ds(pair * 48 + 24 * t, 24), :] = part[:24] + sign * pltpu.roll(part[24:], 64, 1)


def backward_x(f, t2b, u):
    @pl.loop(0, 4, unroll=UNROLL["backward_x"])
    def _(block):
        rows = pl.ds(pl.multiple_of(block * 144, 144), 144)
        hi, lo = split(f[rows, :])
        o = dot(jnp.concatenate([hi, lo], 1), t2b[:256, :]) + dot(hi, t2b[256:, :])
        u[0, rows, :] = o[:, :128]
        u[1, rows, :] = o[:, 128:]


def backward_y(fields, t1b, orbitals, total, fresh, tile):
    @pl.loop(tile * 4, tile * 4 + 4, unroll=UNROLL["backward_y"])
    def _(pair):
        terms = [None, None]
        for u, orbital in zip(fields, orbitals):
            parts = []
            for t in range(2):
                where = pl.ds(pair * 2 + t, HALF, stride=PLANES)
                parts.append(jnp.concatenate([u.at[0][where, :], u.at[1][where, :]], 0))
            hi, lo = split(jnp.concatenate(parts, 1))
            v = dot(t1b[...], jnp.concatenate([hi, lo, hi], 0))
            for t in range(2):
                rows = pl.ds(pl.multiple_of((pair * 2 + t) * PITCH, PITCH), NG)
                term = orbital[rows, :] * v[:, 128 * t : 128 * t + 128]
                terms[t] = term if terms[t] is None else terms[t] + term
        for t in range(2):
            rows = pl.ds(pl.multiple_of((pair * 2 + t) * PITCH, PITCH), NG)
            total[rows, :] = terms[t] if fresh else total[rows, :] + terms[t]


def fill_coulomb(depth, pick, coulomb, limits):
    kept = depth[...].astype(F32)[:HALF] + 1.0
    limits[...] = lax.dot_general(
        kept, pick[...], (((0,), (0,)), ((), ())), preferred_element_type=F32
    ) - 1.0
    lane = lax.broadcasted_iota(jnp.int32, (ROWS, 128), 1) % 64
    row = lax.broadcasted_iota(jnp.int32, (ROWS, 128), 0)
    kx, kz = (lane + 1) // 2, (row + 1) // 2
    square = (kx * kx + kz * kz).astype(F32)
    size = kz.astype(F32)

    @pl.loop(0, HALF, unroll=4)
    def _(ky):
        whole = square + (ky * ky).astype(F32)
        inside = (size <= limits[pl.ds(ky, 1), :]) & (whole > 0.5)
        coulomb[pl.ds(pl.multiple_of(ky * ROWS, ROWS), ROWS), :] = jnp.where(
            inside, COULOMB * NG**1.5 / jnp.maximum(whole, 1.0), 0.0
        )


def kernel(
    own_hbm, depth_hbm, t1_hbm, t2_hbm, t3_hbm, t3b_hbm, t2b_hbm, t1b_hbm, pick_hbm, out,
    own, depth, t1, t2, t3, t3b, t2b, t1b, pick, load_sem, raw, grids, total, u, u2, f, coulomb, limits,
    spectra, arrived, summed, passing, crossed, fields,
    phi_send, phi_recv, half_send, half_recv, far_send, far_recv, aside_send, aside_recv, give_send, give_recv,
):
    orb, fft = lax.axis_index("orb"), lax.axis_index("fft")
    blocks = lax.axis_size("orb")
    core = fft % 2
    other = fft + 1 - 2 * core
    far = (fft + 2) % 4
    near = (orb + blocks - 1 + 2 * core) % blocks
    back = (orb + 1 - 2 * core) % blocks
    aside = orb + 1 - 2 * (orb % 2)
    inner = (orb % 4 + 1) % 4 >= 2

    def distant(place_on_ring):
        return place_on_ring % 16 == 15 * core

    def straight(place):
        return inner | distant(orb) if place and STRAIGHT else inner

    def relays(place):
        return inner & jnp.logical_not(distant(aside)) if place and STRAIGHT else inner

    loads = [
        pltpu.make_async_copy(src, dst, load_sem.at[place])
        for place, (src, dst) in enumerate((
            (own_hbm, own), (depth_hbm, depth), (pick_hbm, pick), (t1_hbm, t1), (t2_hbm, t2),
            (t3_hbm.at[fft], t3), (t3b_hbm.at[fft], t3b), (t2b_hbm, t2b), (t1b_hbm, t1b),
        ))
    ]
    for load in loads:
        load.start()

    barrier = pltpu.get_barrier_semaphore()
    for peer in ((near, fft), (back, fft), (orb, other), (near, other), (orb, far), (aside, far)):
        pl.semaphore_signal(barrier, inc=1, device_id=peer, device_id_type=MESH)
    pl.semaphore_wait(barrier, 6)

    def send(src, dst, send_sem, recv_sem, peer):
        return pltpu.make_async_remote_copy(
            src_ref=src, dst_ref=dst, send_sem=send_sem, recv_sem=recv_sem,
            device_id=peer, device_id_type=MESH,
        )

    def orbital_copy(phase, part, size, peer):
        rows = pl.ds(part * size, size)
        return send(own_hbm.at[rows], raw.at[phase, rows], phi_send.at[phase, part],
                    phi_recv.at[phase, part], peer)

    first = [orbital_copy(0, part, 576, (back, fft)) for part in range(3)]
    second = [orbital_copy(1, part, 1728 // PARTS, (near, fft)) for part in range(PARTS)]
    def follow(when):
        for part in range(PARTS):
            if SECOND[part] == when:
                second[part].start()

    for copy in first:
        copy.start()
    follow("a")

    mine, mate, after = grids.at[0], grids.at[1], grids.at[2]
    chunks = [(0, pl.ds(0, PACKED))] + [(1, pl.ds(PACKED // CHUNKS * k, PACKED // CHUNKS)) for k in range(CHUNKS)]
    peers = [(orb, other)] + [(near, other)] * CHUNKS
    halves = [
        send(spectra.at[pair, 1 - core, rows], arrived.at[pair, rows],
             half_send.at[place], half_recv.at[place], peers[place])
        for place, (pair, rows) in enumerate(chunks)
    ]
    fars = [
        send(summed.at[pair, rows], crossed.at[pair, rows],
             far_send.at[place], far_recv.at[place], (orb, far))
        for place, (pair, rows) in enumerate(chunks)
    ]

    asides = [
        send(summed.at[pair, rows], passing.at[pair, rows],
             aside_send.at[place], aside_recv.at[place], (aside, fft))
        for place, (pair, rows) in enumerate(chunks)
    ]
    onward = [
        send(passing.at[pair, rows], crossed.at[pair, rows],
             aside_send.at[place], far_recv.at[place], (aside, far))
        for place, (pair, rows) in enumerate(chunks)
    ]

    def give(place, slot, field, half, peer):
        pair, rows = chunks[place]
        return send(fields.at[pair, half, rows], fields.at[field, half, rows],
                    give_send.at[place, slot], give_recv.at[place, slot], peer)

    gives = [[give(0, 0, 0, core, (orb, other))]]
    for place in range(1, CHUNKS + 1):
        gives.append([give(place, 0, 1, core, (near, other)), give(place, 1, 2, core, (orb, other)),
                      give(place, 2, 2, core, (near, fft)) if DIRECT else give(place, 2, 2, 1 - core, (orb, other))])

    def cross(place):
        pair, rows = chunks[place]
        halves[place].wait_recv()
        summed[pair, rows] = spectra[pair, core, rows] + arrived[pair, rows]
        if place in ASIDE:
            pl.when(straight(place))(fars[place].start)
            pl.when(jnp.logical_not(straight(place)))(asides[place].start)
        else:
            fars[place].start()

    def pass_on(place):
        if place in ASIDE:
            @pl.when(relays(place))
            def _():
                asides[place].wait_recv()
                onward[place].start()

    def hand_out(place):
        pair, rows = chunks[place]
        fars[place].wait_recv()
        fields[pair, core, rows] = summed[pair, rows] + crossed[pair, rows]
        for copy in gives[place] if DIRECT else gives[place][:2]:
            copy.start()

    for load in loads:
        load.wait()
    fill_coulomb(depth, pick, coulomb, limits)
    for tile in range(3):
        spread(own, mine, tile)
        forward_y(mine, mine, t1, u, tile)
        forward_x(u, t2, f, tile)
    forward_z(f, t3, coulomb, spectra.at[0])
    halves[0].start()
    if OWN_CROSS == "early":
        cross(0)

    for tile in range(3):
        first[tile].wait_recv()
        if tile == 2:
            if OWN_CROSS == "arrived":
                cross(0)
            follow("b")
        spread(raw.at[0], mate, tile)
        forward_y(mine, mate, t1, u, tile)
        forward_x(u, t2, f, tile)
    forward_z(f, t3, coulomb, spectra.at[1])
    if PASS_OWN == "sent":
        pass_on(0)
    for place in range(1, CHUNKS + 1):
        halves[place].start()
    follow("c")
    if OWN_CROSS == "sent":
        cross(0)
    for place in range(1, CHUNKS + 1):
        cross(place)
    if OWN_CROSS == "last":
        cross(0)
    follow("d")
    if PASS_OWN == "crossed":
        pass_on(0)
    for place in range(1, CHUNKS + 1):
        pass_on(place)

    hand_out(0)
    gives[0][0].wait_recv()
    backward_z(fields.at[0], t3b, f)
    backward_x(f, t2b, u)
    for tile in range(3):
        backward_y((u,), t1b, (mine,), total, True, tile)

    for place in range(1, CHUNKS + 1):
        hand_out(place)
        if place == 1:
            follow("e")

    def arrive(when):
        if SPREAD == when:
            for tile in range(3):
                for part in range(PARTS):
                    if part * 3 // PARTS == tile:
                        second[part].wait_recv()
                spread(raw.at[1], after, tile)

    arrive("first")
    for place in range(1, CHUNKS + 1):
        gives[place][0].wait_recv()
        if not DIRECT:
            gives[place][2].start()
    arrive("second")
    backward_z(fields.at[1], t3b, f)
    backward_x(f, t2b, u)
    arrive("third")
    for place in range(1, CHUNKS + 1):
        gives[place][1].wait_recv()
        gives[place][2].wait_recv()
    backward_z(fields.at[2], t3b, f)
    backward_x(f, t2b, u2)
    arrive("last")
    for tile in range(3):
        backward_y((u, u2), t1b, (mate, after), total, False, tile)
        gather(total, out, tile)
    for copy in first + second + halves + sum(gives, []):
        copy.wait_send()
    for place in range(CHUNKS + 1):
        if place in ASIDE:
            pl.when(straight(place))(fars[place].wait_send)
            pl.when(relays(place))(onward[place].wait_send)
            pl.when(jnp.logical_not(straight(place)))(asides[place].wait_send)
        else:
            fars[place].wait_send()


def shards(orbitals, sphere_depth):
    t1, t2, t3, t3b, t2b, t1b, pick = make_tables()
    vmem = pl.BlockSpec(memory_space=pltpu.VMEM)
    cells = PLANES * NG * NG // 128
    dma = pltpu.SemaphoreType.DMA
    tiled = orbitals.reshape(PLANES // 8, 8, NG * NG // 128, 128).transpose(0, 2, 1, 3).reshape(cells, 128)
    result = pl.pallas_call(
        kernel,
        out_shape=pltpu.VMEM((cells, 128), F32),
        in_specs=[pl.BlockSpec(memory_space=pltpu.HBM)] * 9,
        out_specs=vmem,
        scratch_shapes=[
            pltpu.VMEM((cells, 128), F32),
            pltpu.VMEM(sphere_depth.shape, jnp.int32),
            pltpu.VMEM(t1.shape, BF),
            pltpu.VMEM(t2.shape, BF),
            pltpu.VMEM(t3.shape[1:], BF),
            pltpu.VMEM(t3b.shape[1:], BF),
            pltpu.VMEM(t2b.shape, BF),
            pltpu.VMEM(t1b.shape, BF),
            pltpu.VMEM(pick.shape, F32),
            dma((9,)),
            pltpu.VMEM((2, cells, 128), F32),
            pltpu.VMEM((3, (PLANES + 1) * PITCH, 128), F32),
            pltpu.VMEM(((PLANES + 1) * PITCH, 128), F32),
            pltpu.VMEM((2, (HALF + 1) * PLANES, 128), F32),
            pltpu.VMEM((2, (HALF + 1) * PLANES, 128), F32),
            pltpu.VMEM((HALF * PLANES, 128), F32),
            pltpu.VMEM((HALF * ROWS, 128), F32),
            pltpu.VMEM((NG, 128), F32),
            pltpu.VMEM((2, 2, PACKED, 128), F32),
            pltpu.VMEM((2, PACKED, 128), F32),
            pltpu.VMEM((2, PACKED, 128), F32),
            pltpu.VMEM((2, PACKED, 128), F32),
            pltpu.VMEM((2, PACKED, 128), F32),
            pltpu.VMEM((3, 2, PACKED, 128), F32),
            *[dma((2, max(PARTS, 3)))] * 2, *[dma((CHUNKS + 1,))] * 6, *[dma((CHUNKS + 1, 3))] * 2,
        ],
        compiler_params=pltpu.CompilerParams(
            collective_id=0, has_side_effects=True, vmem_limit_bytes=60 << 20
        ),
        cost_estimate=pl.CostEstimate(flops=10**9, bytes_accessed=4 * 10**6, transcendentals=0),
    )(
        tiled, sphere_depth,
        jnp.asarray(t1), jnp.asarray(t2), jnp.asarray(t3), jnp.asarray(t3b),
        jnp.asarray(t2b), jnp.asarray(t1b), jnp.asarray(pick),
    )
    result = result.reshape(PLANES // 8, NG * NG // 128, 8, 128)
    return result.transpose(0, 2, 1, 3).reshape(orbitals.shape)


def solution(mesh):
    placed = (P("orb", "fft", None), P())
    return jax.shard_map(
        shards, mesh=mesh, in_specs=placed, out_specs=P("orb", "fft", None), check_vma=False
    )
```

```python
import functools
import math

import jax
import jax.numpy as jnp
import ml_dtypes
import numpy as np
from jax import lax
from jax.experimental import pallas as pl
from jax.experimental.pallas import tpu as pltpu
from jax.sharding import PartitionSpec as P

NG = 96
PLANES = 24
HALF = 24
PITCH = 104
ROWS = 48
CROP = 23
UNROLL = dict(spread=24, gather=24, forward_y=4, backward_x=4, backward_y=4)
COULOMB = 0.1
BF = jnp.bfloat16
F32 = jnp.float32
MESH = pl.DeviceIdType.MESH


def signed_order(count):
    place = np.arange(count)
    size = (place + 1) // 2
    return np.where(place % 2 == 1, size, -size)


def angle(a, b):
    return 2.0 * math.pi / NG * (np.outer(a, b) % NG)


def half_of(ky):
    return int(ky % 4 in (1, 2))


def pack_blocks():
    place, most = {}, 0
    for half in range(2):
        filled = 0
        for ky in range(HALF):
            for m in range(ROWS // 8):
                left = CROP**2 - ky**2 - (4 * m) ** 2
                if half_of(ky) != half or left < 0:
                    continue
                width = 2 * math.isqrt(left) + 1
                tile, start = divmod(filled, 64)
                end = start + width
                place[ky, m] = [(half, tile, start, start, min(end, 64))]
                if end > 64:
                    place[ky, m].append((half, tile + 1, start + 64, 0, end - 64))
                filled += width
        most = max(most, -(-filled // 64))
    return place, most


PLACE, TILES = pack_blocks()
PACKED = TILES * 8
OWN_CROSS = "early"
STRAIGHT = False
OWN_LATE = True
DIRECT = True
PARTS = 3
SECOND = "ccc"
CHUNKS = 5
SPREAD = "first"
ASIDE = (0, 1, 2, 3, 4)
PASS_OWN = "crossed"


def split_table(table):
    high = table.astype(ml_dtypes.bfloat16)
    low = (table - high.astype(np.float64)).astype(ml_dtypes.bfloat16)
    return high, low


def make_tables():
    grid = np.arange(NG)
    ky = np.arange(HALF)
    a = angle(ky, grid)
    hi, lo = split_table(np.concatenate([np.cos(a), -np.sin(a)], 0))
    t1 = np.block([[hi, hi], [lo, lo]])

    kx = signed_order(47)
    a = np.zeros((128, 64))
    c, s = np.zeros((128, 64)), np.zeros((128, 64))
    c[:NG, :47] = np.cos(angle(grid, kx))
    s[:NG, :47] = np.sin(angle(grid, kx))
    hi, lo = split_table(np.block([[c, -s], [s, c]]))
    t2 = np.concatenate([hi, lo], 1)
    hi, lo = split_table(np.block([[c.T, s.T], [-s.T, c.T]]))
    t2b = np.concatenate([hi, hi, lo], 0)

    weight = np.where(ky == 0, 1.0, 2.0) / float(NG**3)
    a = angle(grid, ky)
    hi, lo = split_table(np.concatenate([np.cos(a) * weight, -np.sin(a) * weight], 1))
    t1b = np.concatenate([hi, hi, lo], 1)

    kz = signed_order(ROWS)
    t3, t3b = [], []
    for slab in range(NG // PLANES):
        z = slab * PLANES + np.arange(PLANES)
        a = angle(kz, z)
        hi, lo = split_table(np.concatenate([np.cos(a), np.sin(a)], 0))
        t3.append(np.concatenate([hi, hi, lo, lo], 1))
        a = angle(z, kz)
        hi, lo = split_table(np.concatenate([np.cos(a), np.sin(a)], 0))
        t3b.append(np.concatenate([hi, hi, lo], 1))
    pick = np.zeros((HALF, 128), np.float32)
    for lane in range(128):
        if lane % 64 < 47:
            pick[abs(kx[lane % 64]), lane] = 1.0
    return t1, t2, np.stack(t3), np.stack(t3b), t2b, t1b, pick


def lanes(rows):
    return lax.broadcasted_iota(jnp.int32, (rows, 128), 1)


def split(value):
    high = value.astype(BF)
    return high, (value - high.astype(F32)).astype(BF)


def dot(a, b):
    return jnp.dot(a, b, preferred_element_type=F32)


def spread(raw, grid, tile):
    row = tile * 8
    lane = lanes(8)

    @pl.loop(0, NG // 4, unroll=UNROLL["spread"])
    def _(group):
        start = tile * 576 + pl.multiple_of(group * 24, 24)
        t0, t1, t2 = [raw[pl.ds(start + 8 * k, 8), :] for k in range(3)]
        pieces = (
            t0,
            pltpu.roll(jnp.where(lane >= 96, t0, t1), 32, 1),
            pltpu.roll(jnp.where(lane >= 64, t1, t2), 64, 1),
            pltpu.roll(t2, 96, 1),
        )
        for j, piece in enumerate(pieces):
            grid[pl.ds(row * PITCH + group * 4 + j, 8, stride=PITCH), :] = piece


def gather(grid, out, tile):
    lane = lanes(8)

    @pl.loop(0, NG // 4, unroll=UNROLL["gather"])
    def _(group):
        a = [grid[pl.ds(tile * 8 * PITCH + group * 4 + j, 8, stride=PITCH), :] for j in range(4)]
        r1, r2, r3 = pltpu.roll(a[1], 96, 1), pltpu.roll(a[2], 64, 1), pltpu.roll(a[3], 32, 1)
        start = tile * 576 + pl.multiple_of(group * 24, 24)
        out[pl.ds(start, 8), :] = jnp.where(lane < 96, a[0], r1)
        out[pl.ds(start + 8, 8), :] = jnp.where(lane < 64, r1, r2)
        out[pl.ds(start + 16, 8), :] = jnp.where(lane < 32, r2, r3)


def forward_y(left, right, t1, u, tile):
    @pl.loop(tile * 4, tile * 4 + 4, unroll=UNROLL["forward_y"])
    def _(pair):
        planes = [pl.ds(pl.multiple_of((pair * 2 + t) * PITCH, PITCH), NG) for t in range(2)]
        hi, lo = split(jnp.concatenate([left[rows, :] * right[rows, :] for rows in planes], 1))
        o = dot(t1[...], jnp.concatenate([hi, lo], 0))
        o = o[:48] + o[48:]
        for t in range(2):
            where = pl.ds(pair * 2 + t, HALF, stride=PLANES)
            u.at[0][where, :] = o[:24, 128 * t : 128 * t + 128]
            u.at[1][where, :] = o[24:, 128 * t : 128 * t + 128]


def forward_x(u, t2, f, tile):
    places = [pl.ds(ky * PLANES + tile * 8, 8) for ky in range(HALF)]
    parts = [jnp.concatenate([u[c, where, :] for where in places], 0) for c in range(2)]
    hi, lo = split(jnp.concatenate(parts, 1))
    o = dot(hi, t2[...])
    o = o[:, :128] + o[:, 128:] + dot(lo, t2[:, :128])
    for ky, where in enumerate(places):
        f[where, :] = o[8 * ky : 8 * ky + 8]


def forward_z(f, t3, coulomb, spectrum):
    sign = jnp.where(lanes(ROWS) < 64, 1.0, -1.0)
    lane = lanes(8) % 64
    written = set()
    for pair in range(HALF // 2):
        v = f[pl.ds(pair * 48, 48), :]
        v = jnp.concatenate([v[:24], v[24:]], 1)
        hi = v.astype(BF).astype(F32)
        lo = v - hi
        o = dot(t3[...], jnp.concatenate([hi, lo, hi, lo], 0).astype(BF))
        for t in range(2):
            ky = pair * 2 + t
            part = o[:, 128 * t : 128 * t + 128]
            part = part[:48] + sign * pltpu.roll(part[48:], 64, 1)
            part = part * coulomb[pl.ds(ky * ROWS, ROWS), :]
            for m in range(ROWS // 8):
                if (ky, m) not in PLACE:
                    continue
                for half, tile, shift, low, high in PLACE[ky, m]:
                    block = part[8 * m : 8 * m + 8]
                    if shift:
                        block = pltpu.roll(block, shift, 1)
                    if len(PLACE[ky, m]) > 1:
                        block = jnp.where((lane >= low) & (lane < high), block, 0.0)
                    rows = pl.ds(tile * 8, 8)
                    if (half, tile) in written:
                        block = block + spectrum[half, rows, :]
                    spectrum[half, rows, :] = block
                    written.add((half, tile))
    for half in range(2):
        for tile in range(TILES):
            if (half, tile) not in written:
                spectrum[half, pl.ds(tile * 8, 8), :] = jnp.zeros((8, 128), F32)


def backward_z(spectrum, t3b, f):
    sign = jnp.where(lanes(PLANES) < 64, -1.0, 1.0)
    lane = lanes(8) % 64
    none = jnp.zeros((8, 128), F32)

    def unpacked(ky):
        blocks = []
        for m in range(ROWS // 8):
            if (ky, m) not in PLACE:
                blocks.append(none)
                continue
            total = None
            for half, tile, shift, low, high in PLACE[ky, m]:
                block = jnp.where((lane >= low) & (lane < high), spectrum[half, pl.ds(tile * 8, 8), :], 0.0)
                if shift:
                    block = pltpu.roll(block, 128 - shift, 1)
                total = block if total is None else total + block
            blocks.append(total)
        return jnp.concatenate(blocks, 0)

    for pair in range(HALF // 2):
        hi, lo = split(jnp.concatenate([unpacked(pair * 2), unpacked(pair * 2 + 1)], 1))
        o = dot(t3b[...], jnp.concatenate([hi, lo, hi], 0))
        for t in range(2):
            part = o[:, 128 * t : 128 * t + 128]
            f[pl.ds(pair * 48 + 24 * t, 24), :] = part[:24] + sign * pltpu.roll(part[24:], 64, 1)


def backward_x(f, t2b, u):
    @pl.loop(0, 4, unroll=UNROLL["backward_x"])
    def _(block):
        rows = pl.ds(pl.multiple_of(block * 144, 144), 144)
        hi, lo = split(f[rows, :])
        o = dot(jnp.concatenate([hi, lo], 1), t2b[:256, :]) + dot(hi, t2b[256:, :])
        u[0, rows, :] = o[:, :128]
        u[1, rows, :] = o[:, 128:]


def backward_y(fields, t1b, orbitals, total, fresh, tile):
    @pl.loop(tile * 4, tile * 4 + 4, unroll=UNROLL["backward_y"])
    def _(pair):
        terms = [None, None]
        for u, orbital in zip(fields, orbitals):
            parts = []
            for t in range(2):
                where = pl.ds(pair * 2 + t, HALF, stride=PLANES)
                parts.append(jnp.concatenate([u.at[0][where, :], u.at[1][where, :]], 0))
            hi, lo = split(jnp.concatenate(parts, 1))
            v = dot(t1b[...], jnp.concatenate([hi, lo, hi], 0))
            for t in range(2):
                rows = pl.ds(pl.multiple_of((pair * 2 + t) * PITCH, PITCH), NG)
                term = orbital[rows, :] * v[:, 128 * t : 128 * t + 128]
                terms[t] = term if terms[t] is None else terms[t] + term
        for t in range(2):
            rows = pl.ds(pl.multiple_of((pair * 2 + t) * PITCH, PITCH), NG)
            total[rows, :] = terms[t] if fresh else total[rows, :] + terms[t]


def fill_coulomb(depth, pick, coulomb, limits):
    kept = depth[...].astype(F32)[:HALF] + 1.0
    limits[...] = lax.dot_general(
        kept, pick[...], (((0,), (0,)), ((), ())), preferred_element_type=F32
    ) - 1.0
    lane = lax.broadcasted_iota(jnp.int32, (ROWS, 128), 1) % 64
    row = lax.broadcasted_iota(jnp.int32, (ROWS, 128), 0)
    kx, kz = (lane + 1) // 2, (row + 1) // 2
    square = (kx * kx + kz * kz).astype(F32)
    size = kz.astype(F32)

    @pl.loop(0, HALF, unroll=4)
    def _(ky):
        whole = square + (ky * ky).astype(F32)
        inside = (size <= limits[pl.ds(ky, 1), :]) & (whole > 0.5)
        coulomb[pl.ds(pl.multiple_of(ky * ROWS, ROWS), ROWS), :] = jnp.where(
            inside, COULOMB * NG**1.5 / jnp.maximum(whole, 1.0), 0.0
        )


def kernel(
    own_hbm, depth_hbm, t1_hbm, t2_hbm, t3_hbm, t3b_hbm, t2b_hbm, t1b_hbm, pick_hbm, out,
    own, depth, t1, t2, t3, t3b, t2b, t1b, pick, load_sem, raw, grids, total, u, u2, f, coulomb, limits,
    spectra, arrived, summed, passing, crossed, fields,
    phi_send, phi_recv, half_send, half_recv, far_send, far_recv, aside_send, aside_recv, give_send, give_recv,
):
    orb, fft = lax.axis_index("orb"), lax.axis_index("fft")
    blocks = lax.axis_size("orb")
    core = fft % 2
    other = fft + 1 - 2 * core
    far = (fft + 2) % 4
    near = (orb + blocks - 1 + 2 * core) % blocks
    back = (orb + 1 - 2 * core) % blocks
    aside = orb + 1 - 2 * (orb % 2)
    inner = (orb % 4 + 1) % 4 >= 2

    def distant(place_on_ring):
        return place_on_ring % 16 == 15 * core

    def straight(place):
        return inner | distant(orb) if place and STRAIGHT else inner

    def relays(place):
        return inner & jnp.logical_not(distant(aside)) if place and STRAIGHT else inner

    loads = [
        pltpu.make_async_copy(src, dst, load_sem.at[place])
        for place, (src, dst) in enumerate((
            (own_hbm, own), (depth_hbm, depth), (pick_hbm, pick), (t1_hbm, t1), (t2_hbm, t2),
            (t3_hbm.at[fft], t3), (t3b_hbm.at[fft], t3b), (t2b_hbm, t2b), (t1b_hbm, t1b),
        ))
    ]
    for load in loads:
        load.start()

    barrier = pltpu.get_barrier_semaphore()
    for peer in ((near, fft), (back, fft), (orb, other), (near, other), (orb, far), (aside, far)):
        pl.semaphore_signal(barrier, inc=1, device_id=peer, device_id_type=MESH)
    pl.semaphore_wait(barrier, 6)

    def send(src, dst, send_sem, recv_sem, peer):
        return pltpu.make_async_remote_copy(
            src_ref=src, dst_ref=dst, send_sem=send_sem, recv_sem=recv_sem,
            device_id=peer, device_id_type=MESH,
        )

    def orbital_copy(phase, part, size, peer):
        rows = pl.ds(part * size, size)
        return send(own_hbm.at[rows], raw.at[phase, rows], phi_send.at[phase, part],
                    phi_recv.at[phase, part], peer)

    first = [orbital_copy(0, part, 576, (back, fft)) for part in range(3)]
    second = [orbital_copy(1, part, 1728 // PARTS, (near, fft)) for part in range(PARTS)]
    def follow(when):
        for part in range(PARTS):
            if SECOND[part] == when:
                second[part].start()

    for copy in first:
        copy.start()
    follow("a")

    mine, mate, after = grids.at[0], grids.at[1], grids.at[2]
    chunks = [(0, pl.ds(0, PACKED))] + [(1, pl.ds(PACKED // CHUNKS * k, PACKED // CHUNKS)) for k in range(CHUNKS)]
    peers = [(orb, other)] + [(near, other)] * CHUNKS
    halves = [
        send(spectra.at[pair, 1 - core, rows], arrived.at[pair, rows],
             half_send.at[place], half_recv.at[place], peers[place])
        for place, (pair, rows) in enumerate(chunks)
    ]
    fars = [
        send(summed.at[pair, rows], crossed.at[pair, rows],
             far_send.at[place], far_recv.at[place], (orb, far))
        for place, (pair, rows) in enumerate(chunks)
    ]

    asides = [
        send(summed.at[pair, rows], passing.at[pair, rows],
             aside_send.at[place], aside_recv.at[place], (aside, fft))
        for place, (pair, rows) in enumerate(chunks)
    ]
    onward = [
        send(passing.at[pair, rows], crossed.at[pair, rows],
             aside_send.at[place], far_recv.at[place], (aside, far))
        for place, (pair, rows) in enumerate(chunks)
    ]

    def give(place, slot, field, half, peer):
        pair, rows = chunks[place]
        return send(fields.at[pair, half, rows], fields.at[field, half, rows],
                    give_send.at[place, slot], give_recv.at[place, slot], peer)

    gives = [[give(0, 0, 0, core, (orb, other))]]
    for place in range(1, CHUNKS + 1):
        gives.append([give(place, 0, 1, core, (near, other)), give(place, 1, 2, core, (orb, other)),
                      give(place, 2, 2, core, (near, fft)) if DIRECT else give(place, 2, 2, 1 - core, (orb, other))])

    def cross(place):
        pair, rows = chunks[place]
        halves[place].wait_recv()
        summed[pair, rows] = spectra[pair, core, rows] + arrived[pair, rows]
        if place in ASIDE:
            pl.when(straight(place))(fars[place].start)
            pl.when(jnp.logical_not(straight(place)))(asides[place].start)
        else:
            fars[place].start()

    def pass_on(place):
        if place in ASIDE:
            @pl.when(relays(place))
            def _():
                asides[place].wait_recv()
                onward[place].start()

    def hand_out(place):
        pair, rows = chunks[place]
        fars[place].wait_recv()
        fields[pair, core, rows] = summed[pair, rows] + crossed[pair, rows]
        for copy in gives[place] if DIRECT else gives[place][:2]:
            copy.start()

    for load in loads:
        load.wait()
    fill_coulomb(depth, pick, coulomb, limits)
    for tile in range(3):
        spread(own, mine, tile)
        forward_y(mine, mine, t1, u, tile)
        forward_x(u, t2, f, tile)
    forward_z(f, t3, coulomb, spectra.at[0])
    halves[0].start()
    if OWN_CROSS == "early":
        cross(0)

    for tile in range(3):
        if PASS_OWN == tile:
            pass_on(0)
        first[tile].wait_recv()
        if tile == 2:
            if OWN_CROSS == "arrived":
                cross(0)
            follow("b")
        spread(raw.at[0], mate, tile)
        forward_y(mine, mate, t1, u, tile)
        forward_x(u, t2, f, tile)
    forward_z(f, t3, coulomb, spectra.at[1])
    if PASS_OWN == "sent":
        pass_on(0)
    for place in range(1, CHUNKS + 1):
        halves[place].start()
    follow("c")
    if OWN_CROSS == "sent":
        cross(0)
    for place in range(1, CHUNKS + 1):
        cross(place)
    if OWN_CROSS == "last":
        cross(0)
    follow("d")
    if PASS_OWN == "crossed":
        pass_on(0)
    for place in range(1, CHUNKS + 1):
        pass_on(place)

    def finish_own():
        hand_out(0)
        gives[0][0].wait_recv()
        backward_z(fields.at[0], t3b, f)
        backward_x(f, t2b, u)
        for tile in range(3):
            backward_y((u,), t1b, (mine,), total, True, tile)

    if not OWN_LATE:
        finish_own()

    for place in range(1, CHUNKS + 1):
        hand_out(place)
        if place == 1:
            follow("e")
    if OWN_LATE:
        finish_own()

    def arrive(when):
        if SPREAD == when:
            for tile in range(3):
                for part in range(PARTS):
                    if part * 3 // PARTS == tile:
                        second[part].wait_recv()
                spread(raw.at[1], after, tile)

    arrive("first")
    for place in range(1, CHUNKS + 1):
        gives[place][0].wait_recv()
        if not DIRECT:
            gives[place][2].start()
    arrive("second")
    backward_z(fields.at[1], t3b, f)
    backward_x(f, t2b, u)
    arrive("third")
    for place in range(1, CHUNKS + 1):
        gives[place][1].wait_recv()
        gives[place][2].wait_recv()
    backward_z(fields.at[2], t3b, f)
    backward_x(f, t2b, u2)
    arrive("last")
    for tile in range(3):
        backward_y((u, u2), t1b, (mate, after), total, False, tile)
        gather(total, out, tile)
    for copy in first + second + halves + sum(gives, []):
        copy.wait_send()
    for place in range(CHUNKS + 1):
        if place in ASIDE:
            pl.when(straight(place))(fars[place].wait_send)
            pl.when(relays(place))(onward[place].wait_send)
            pl.when(jnp.logical_not(straight(place)))(asides[place].wait_send)
        else:
            fars[place].wait_send()


def shards(orbitals, sphere_depth):
    t1, t2, t3, t3b, t2b, t1b, pick = make_tables()
    vmem = pl.BlockSpec(memory_space=pltpu.VMEM)
    cells = PLANES * NG * NG // 128
    dma = pltpu.SemaphoreType.DMA
    tiled = orbitals.reshape(PLANES // 8, 8, NG * NG // 128, 128).transpose(0, 2, 1, 3).reshape(cells, 128)
    result = pl.pallas_call(
        kernel,
        out_shape=pltpu.VMEM((cells, 128), F32),
        in_specs=[pl.BlockSpec(memory_space=pltpu.HBM)] * 9,
        out_specs=vmem,
        scratch_shapes=[
            pltpu.VMEM((cells, 128), F32),
            pltpu.VMEM(sphere_depth.shape, jnp.int32),
            pltpu.VMEM(t1.shape, BF),
            pltpu.VMEM(t2.shape, BF),
            pltpu.VMEM(t3.shape[1:], BF),
            pltpu.VMEM(t3b.shape[1:], BF),
            pltpu.VMEM(t2b.shape, BF),
            pltpu.VMEM(t1b.shape, BF),
            pltpu.VMEM(pick.shape, F32),
            dma((9,)),
            pltpu.VMEM((2, cells, 128), F32),
            pltpu.VMEM((3, (PLANES + 1) * PITCH, 128), F32),
            pltpu.VMEM(((PLANES + 1) * PITCH, 128), F32),
            pltpu.VMEM((2, (HALF + 1) * PLANES, 128), F32),
            pltpu.VMEM((2, (HALF + 1) * PLANES, 128), F32),
            pltpu.VMEM((HALF * PLANES, 128), F32),
            pltpu.VMEM((HALF * ROWS, 128), F32),
            pltpu.VMEM((NG, 128), F32),
            pltpu.VMEM((2, 2, PACKED, 128), F32),
            pltpu.VMEM((2, PACKED, 128), F32),
            pltpu.VMEM((2, PACKED, 128), F32),
            pltpu.VMEM((2, PACKED, 128), F32),
            pltpu.VMEM((2, PACKED, 128), F32),
            pltpu.VMEM((3, 2, PACKED, 128), F32),
            *[dma((2, max(PARTS, 3)))] * 2, *[dma((CHUNKS + 1,))] * 6, *[dma((CHUNKS + 1, 3))] * 2,
        ],
        compiler_params=pltpu.CompilerParams(
            collective_id=0, has_side_effects=True, vmem_limit_bytes=60 << 20
        ),
        cost_estimate=pl.CostEstimate(flops=10**9, bytes_accessed=4 * 10**6, transcendentals=0),
    )(
        tiled, sphere_depth,
        jnp.asarray(t1), jnp.asarray(t2), jnp.asarray(t3), jnp.asarray(t3b),
        jnp.asarray(t2b), jnp.asarray(t1b), jnp.asarray(pick),
    )
    result = result.reshape(PLANES // 8, NG * NG // 128, 8, 128)
    return result.transpose(0, 2, 1, 3).reshape(orbitals.shape)


def solution(mesh):
    placed = (P("orb", "fft", None), P())
    return jax.shard_map(
        shards, mesh=mesh, in_specs=placed, out_specs=P("orb", "fft", None), check_vma=False
    )
```
